32 devices in a mesh: graph: 4 (over z), feat: 8 (over y, x, core).
Axes of the slice: x: 2, y: 2, z: 4, core: 2. Of those that a mesh axis runs over, the one named last changes fastest.
Arguments:
- node_features: bfloat16 [32768, 1024], P('graph', 'feat'), may hold values from -6 to 6
- proj_weight: bfloat16 [1024, 512], P('feat'), may hold values from -0.1875 to 0.1875
- relation_weight: bfloat16 [2, 512, 512], replicated, may hold values from -0.25 to 0.25
- att_source: float32 [2, 512], replicated, may hold values from -8 to 8
- att_target: float32 [2, 512], replicated, may hold values from -8 to 8
- edge_mask: int32 [256, 12, 128, 128], P(('graph', 'feat')), may hold values from 0 to 1, as said below
- relation_ids: int32 [256, 12], P(('graph', 'feat')), may hold values from 0 to 1
- send_blocks: int32 [32, 4, 4], P(('graph', 'feat')), may hold values from 0 to 7, as said below
- source_slots: int32 [256, 12], P(('graph', 'feat')), may hold values from 0 to 15
Outputs:
- layer_out: bfloat16 [32768, 512], P(('graph', 'feat'))
The draws below stay inside these ranges and needn't reach their ends.
Inputs may be any that keep to these rules, and one draw needn't show every extreme that they name: `edge_mask`: every target row i has an edge at list position 0 to row i of that source block. `send_blocks`: the 4 entries of one device's list to one graph index are distinct block numbers of that device.
All inputs are finite; a program needn't handle non-finite values.
Results may differ from the reference program's by a relative error of at most 0.034.
Values may be sent and summed in bfloat16 or wider, within the bound.
A program may use at most 128 MiB of HBM per device.

```python
import jax
import jax.numpy as jnp
from jax import lax

DIN = 1024
HID = 512
HEADS = 4
BR = 128
REL = 2
BLK_DEV = 8
KSRC = 12
CAP = 4
BLOCKS = 256
NODES = 32768
N_GRAPH = 4
N_FEAT = 8
DEVICES = 32


def draw_att_source(key, part):
    key = jax.random.fold_in(key, 11)
    return jnp.clip(0.18 * jax.random.normal(key, (REL, HID), jnp.float32), -8.0, 8.0)


def draw_att_target(key, part):
    key = jax.random.fold_in(key, 12)
    return jnp.clip(0.18 * jax.random.normal(key, (REL, HID), jnp.float32), -8.0, 8.0)


def draw_edge_mask(key, part):
    key = jax.random.fold_in(key, 13)
    coins = jax.random.randint(key, (BLOCKS, KSRC, BR, BR), 0, KSRC * BR)
    first = (jnp.arange(KSRC) == 0)[None, :, None, None]
    diagonal = (jnp.arange(BR)[:, None] == jnp.arange(BR)[None, :])[None, None]
    return ((coins < 16) | first & diagonal).astype(jnp.int32)


def draw_send_blocks(key, part):
    key = jax.random.fold_in(key, 14)
    keys = jax.random.split(key, DEVICES * N_GRAPH)
    orders = jax.vmap(lambda single: jax.random.permutation(single, BLK_DEV))(keys)
    return orders[:, :CAP].reshape(DEVICES, N_GRAPH, CAP).astype(jnp.int32)


def place_ends(drawn, stream_key, least, high):
    place = [jax.random.randint(jax.random.fold_in(stream_key, axis), (), 0, length) for axis, length in enumerate(drawn.shape)]
    longest = drawn.shape.index(max(drawn.shape))
    beside = place[:longest] + [(place[longest] + 1) % drawn.shape[longest]] + place[longest + 1:]
    return drawn.at[tuple(place)].set(least).at[tuple(beside)].set(high)


def levels(stream_key, dims, pieces, least, largest):
    loudness = 1.0
    for position, blocks in pieces:
        steps = jax.random.uniform(jax.random.fold_in(jax.random.fold_in(stream_key, 6), position), (blocks,), jnp.float32, least / len(pieces), largest / len(pieces))
        loudness = loudness * jnp.repeat(jnp.exp(steps), dims[position] // blocks).reshape((-1,) + (1,) * (len(dims) - 1 - position))
    return loudness


def normal_values(key, dims, deviation, most, pieces=(), kind=jnp.bfloat16):
    values = deviation * jax.random.normal(key, dims, jnp.float32)
    if pieces:
        values = values * levels(key, dims, pieces, -0.22, 0.18)
    return jnp.clip(values, -most, most).astype(kind)


def setup_inputs(seed: int = 0) -> dict:
    seeds = jax.random.split(jax.random.key(seed), 10)
    node_features = normal_values(seeds[0], (NODES, DIN), 1.0, 6.0, ((0, 4), (1, 8)))
    proj_weight = normal_values(seeds[1], (DIN, HID), DIN ** -0.5, 0.1875, ((0, 8),))
    relation_weight = normal_values(seeds[2], (REL, HID, HID), HID ** -0.5, 0.25)
    att_source = draw_att_source(jax.random.fold_in(seeds[9], 71), 0)
    att_target = draw_att_target(jax.random.fold_in(seeds[9], 71), 0)
    edge_mask = draw_edge_mask(jax.random.fold_in(seeds[9], 71), 0)
    relation_ids = place_ends(jax.random.randint(seeds[6], (BLOCKS, KSRC), 0, REL), jax.random.fold_in(seeds[6], 1), 0, REL - 1).astype(jnp.int32)
    send_blocks = draw_send_blocks(jax.random.fold_in(seeds[9], 71), 0)
    source_slots = place_ends(jax.random.randint(seeds[8], (BLOCKS, KSRC), 0, N_GRAPH * CAP), jax.random.fold_in(seeds[8], 1), 0, (N_GRAPH * CAP) - 1).astype(jnp.int32)
    return dict(node_features=node_features, proj_weight=proj_weight, relation_weight=relation_weight, att_source=att_source, att_target=att_target, edge_mask=edge_mask, relation_ids=relation_ids, send_blocks=send_blocks, source_slots=source_slots)


def attend(target_scores, source_scores, live, values, own):
    heads_count = target_scores.shape[1]
    width = values.shape[2]
    lists = target_scores.shape[0]
    rows = target_scores.shape[2]
    lhs = jnp.transpose(target_scores, (1, 2, 0))
    rhs = jnp.transpose(source_scores, (1, 0, 2))
    raw = lhs[:, :, :, None] + rhs[:, None, :, :]
    leaky = jnp.where(raw > 0, raw, 0.2 * raw)
    usable = (jnp.transpose(live, (1, 0, 2)) > 0)[None]
    masked = jnp.where(usable, leaky, -jnp.inf)
    highest = jnp.max(masked, axis=(2, 3), keepdims=True)
    prob = jnp.exp(masked - highest)
    total = jnp.sum(prob, axis=(2, 3))
    weights = prob.astype(jnp.bfloat16).reshape(heads_count, rows, lists * values.shape[1])
    stacked = values.reshape(lists * values.shape[1], heads_count, width // heads_count)
    summed = jnp.einsum("hix,xhd->hid", weights.astype(jnp.float32), stacked.astype(jnp.float32))
    summed = summed / total[:, :, None]
    mixed = jnp.transpose(summed, (1, 0, 2)).reshape(rows, width) + own.astype(jnp.float32)
    return jax.nn.elu(mixed).astype(jnp.bfloat16)


def reference(node_features, proj_weight, relation_weight, att_source, att_target, edge_mask, relation_ids, send_blocks, source_slots):
    head_width = HID // HEADS
    hidden = jnp.dot(node_features, proj_weight, preferred_element_type=jnp.float32).astype(jnp.bfloat16)
    blocks = hidden.reshape(BLOCKS, BR, HID)
    values_all = jnp.stack([jnp.dot(hidden, relation_weight[r], preferred_element_type=jnp.float32).astype(jnp.bfloat16) for r in range(REL)]).reshape(REL, BLOCKS, BR, HID)
    src_heads = values_all.astype(jnp.float32).reshape(REL, BLOCKS, BR, HEADS, head_width)
    source_all = jnp.sum(src_heads * att_source.reshape(REL, 1, 1, HEADS, head_width), axis=-1)
    source_all = jnp.transpose(source_all, (0, 1, 3, 2))
    device_ids = jnp.arange(DEVICES, dtype=jnp.int32)[:, None, None]
    peer_ids = jnp.arange(N_GRAPH, dtype=jnp.int32)[None, :, None]
    slot_ids = jnp.arange(CAP, dtype=jnp.int32)[None, None, :]
    sender = peer_ids * N_FEAT + device_ids % N_FEAT
    frontier = sender * BLK_DEV + send_blocks[sender, device_ids // N_FEAT, slot_ids]
    frontier = frontier.reshape(DEVICES, N_GRAPH * CAP).astype(jnp.int32)
    att_heads = att_target.reshape(REL, HEADS, head_width)

    def one_block(index):
        rels = relation_ids[index]
        sources = frontier[index // BLK_DEV][source_slots[index]]
        chosen = values_all[rels, sources]
        source_scores = source_all[rels, sources]
        own = blocks[index]
        own_heads = own.astype(jnp.float32).reshape(BR, HEADS, head_width)
        target_scores = jnp.sum(own_heads[None] * att_heads[rels][:, None], axis=-1)
        target_scores = jnp.transpose(target_scores, (0, 2, 1))
        return attend(target_scores, source_scores, edge_mask[index], chosen, own)

    result = lax.map(one_block, jnp.arange(BLOCKS, dtype=jnp.int32))
    return result.reshape(NODES, HID)
```

```python
import functools
import math

import jax
import jax.numpy as jnp
from jax import lax
from jax.experimental import pallas as pl
from jax.experimental.pallas import tpu as pltpu
from jax.sharding import PartitionSpec as P

HEADS = 4
LOG2E = math.log2(math.e)
NT = (((1,), (1,)), ((), ()))


def split_bf16(x):
    hi = x.astype(jnp.bfloat16)
    lo = (x - hi.astype(jnp.float32)).astype(jnp.bfloat16)
    return hi, lo


def hidden_kernel(x_ref, w_ref, out_ref):
    total = jnp.dot(x_ref[0], w_ref[0], preferred_element_type=jnp.float32)
    for f in range(1, x_ref.shape[0]):
        total += jnp.dot(x_ref[f], w_ref[f], preferred_element_type=jnp.float32)
    out_ref[...] = total.astype(out_ref.dtype)


def project(x, w):
    feats, rows, depth = x.shape
    width = w.shape[2]
    tile = min(rows, 256)
    return pl.pallas_call(
        hidden_kernel,
        grid=(rows // tile,),
        in_specs=[
            pl.BlockSpec((feats, tile, depth), lambda i: (0, i, 0)),
            pl.BlockSpec((feats, depth, width), lambda i: (0, 0, 0)),
        ],
        out_specs=pl.BlockSpec((tile, width), lambda i: (i, 0)),
        out_shape=jax.ShapeDtypeStruct((rows, width), jnp.bfloat16),
        compiler_params=pltpu.CompilerParams(vmem_limit_bytes=40 << 20),
        name="project",
    )(x, w)


def attention_kernel(
    rels_ref,
    slots_ref,
    front_ref,
    own_ref,
    relw_ref,
    atts_ref,
    attt_ref,
    mask_ref,
    out_ref,
    values,
    scores,
    tatt,
    target,
    stack,
    raws,
    bias,
    weights,
):
    slots = front_ref.shape[0]
    rows = front_ref.shape[1]
    width = front_ref.shape[2]
    hw = width // HEADS
    relations = relw_ref.shape[0]
    lists = mask_ref.shape[1]
    b = pl.program_id(0)

    @pl.when(b == 0)
    def _():
        head_of = lax.broadcasted_iota(jnp.int32, (8, width), 1) // hw
        row_of = lax.broadcasted_iota(jnp.int32, (8, width), 0)
        for r in range(relations):
            hi, lo = split_bf16(atts_ref[r : r + 1, :] * LOG2E)
            parts = [
                jnp.where(head_of == row_of, part.astype(jnp.float32), 0.0)
                for part in (hi, lo)
            ]
            att = jnp.concatenate(parts, axis=0).astype(jnp.bfloat16)

            def one_slot(s, carry):
                v = jnp.dot(
                    front_ref[s], relw_ref[r], preferred_element_type=jnp.float32
                ).astype(jnp.bfloat16)
                values[r * slots + s] = v
                both = lax.dot_general(att, v, NT, preferred_element_type=jnp.float32)
                scores[r * slots + s] = both[:8] + both[8:]
                return carry

            lax.fori_loop(0, slots, one_slot, 0)
            hi, lo = split_bf16(attt_ref[r : r + 1, :] * LOG2E)
            for n, part in enumerate((hi, lo)):
                tatt[n, r * rows : (r + 1) * rows, :] = jnp.broadcast_to(
                    part.astype(jnp.float32), (rows, width)
                ).astype(jnp.bfloat16)
        stack[:, :, hw:] = jnp.ones((HEADS, lists * rows, hw), jnp.bfloat16)

    index = []
    for k in range(lists):
        rel = rels_ref[b, k]
        index.append((rel, rel * slots + slots_ref[b, k]))
    for k in range(lists):
        v = values[index[k][1]]
        for h in range(HEADS):
            stack[h, k * rows : (k + 1) * rows, :hw] = v[:, h * hw : (h + 1) * hw]
        bias[k] = jnp.where(mask_ref[0, k] > 0, 0.0, -jnp.inf)
    for h in range(HEADS):
        cols = slice(h * hw, (h + 1) * hw)
        own = own_ref[:, cols]
        both = lax.dot_general(
            own, tatt[0, :, cols], NT, preferred_element_type=jnp.float32
        ) + lax.dot_general(own, tatt[1, :, cols], NT, preferred_element_type=jnp.float32)
        for r in range(relations):
            target[r] = both[:, r * rows : (r + 1) * rows]
        top = None
        for k in range(lists):
            rel, place = index[k]
            raw = (target[rel] + scores[place, h : h + 1, :]) + bias[k]
            raws[k] = raw
            top = raw if top is None else jnp.maximum(top, raw)
        top = jnp.max(top, axis=1, keepdims=True)
        top = jnp.broadcast_to(jnp.maximum(top, 0.2 * top), (rows, rows))
        for k in range(lists):
            raw = raws[k]
            prob = jnp.exp2(jnp.maximum(raw, 0.2 * raw) - top)
            weights[:, k * rows : (k + 1) * rows] = prob.astype(jnp.bfloat16)
        summed = jnp.dot(weights[...], stack[h], preferred_element_type=jnp.float32)
        mixed = summed[:, :hw] / summed[:, hw:] + own.astype(jnp.float32)
        out_ref[:, cols] = jnp.where(
            mixed > 0, mixed, jnp.exp(jnp.minimum(mixed, 0.0)) - 1.0
        ).astype(out_ref.dtype)


def attention(rels, slots, front, hidden, relw, atts, attt, mask):
    count, rows, width = front.shape
    blocks, lists = mask.shape[:2]
    relations = relw.shape[0]
    hw = width // HEADS
    smem = pl.BlockSpec(memory_space=pltpu.SMEM)
    whole = pl.BlockSpec(memory_space=pltpu.VMEM)
    return pl.pallas_call(
        attention_kernel,
        grid=(blocks,),
        in_specs=[
            smem,
            smem,
            whole,
            pl.BlockSpec((rows, width), lambda b: (b, 0)),
            whole,
            whole,
            whole,
            pl.BlockSpec((1, lists, rows, rows), lambda b: (b, 0, 0, 0)),
        ],
        out_specs=pl.BlockSpec((rows, width), lambda b: (b, 0)),
        out_shape=jax.ShapeDtypeStruct((blocks * rows, width), jnp.bfloat16),
        scratch_shapes=[
            pltpu.VMEM((relations * count, rows, width), jnp.bfloat16),
            pltpu.VMEM((relations * count, 8, rows), jnp.float32),
            pltpu.VMEM((2, relations * rows, width), jnp.bfloat16),
            pltpu.VMEM((relations, rows, rows), jnp.float32),
            pltpu.VMEM((HEADS, lists * rows, 2 * hw), jnp.bfloat16),
            pltpu.VMEM((lists, rows, rows), jnp.float32),
            pltpu.VMEM((lists, rows, rows), jnp.float32),
            pltpu.VMEM((rows, lists * rows), jnp.bfloat16),
        ],
        compiler_params=pltpu.CompilerParams(vmem_limit_bytes=56 << 20),
        name="attention",
    )(rels, slots, front, hidden, relw, atts, attt, mask)


def shards(x, w, relw, atts, attt, mask, rels, send, slots):
    rows = mask.shape[-1]
    blocks = mask.shape[0]
    feats = x.shape[0] // (blocks * rows)
    x = x.reshape(feats, blocks * rows, x.shape[1])
    x = lax.all_to_all(x, "feat", split_axis=0, concat_axis=0, tiled=True)
    w = lax.all_gather(w, "feat", axis=0)
    hidden = project(x, w)
    out = hidden.reshape(blocks, rows, -1)[send[0]]
    front = lax.all_to_all(out, "graph", split_axis=0, concat_axis=0, tiled=True)
    front = front.reshape((-1,) + front.shape[2:])
    return attention(rels, slots, front, hidden, relw, atts, attt, mask)


def solution(mesh):
    placed = (
        P("graph", "feat"),
        P("feat", None),
        P(),
        P(),
        P(),
        P(("graph", "feat"), None, None, None),
        P(("graph", "feat"), None),
        P(("graph", "feat"), None, None),
        P(("graph", "feat"), None),
    )
    return jax.shard_map(
        shards, mesh=mesh, in_specs=placed, out_specs=P(("graph", "feat"), None), check_vma=False
    )
```

```python
import functools
import math

import jax
import jax.numpy as jnp
from jax import lax
from jax.experimental import pallas as pl
from jax.experimental.pallas import tpu as pltpu
from jax.sharding import PartitionSpec as P

HEADS = 4
AHEAD = 3
LOG2E = math.log2(math.e)
NT = (((1,), (1,)), ((), ()))


def split_bf16(x):
    hi = x.astype(jnp.bfloat16)
    lo = (x - hi.astype(jnp.float32)).astype(jnp.bfloat16)
    return hi, lo


def exchange_kernel(
    x_ref,
    w_ref,
    send_ref,
    gat,
    sends,
    xg,
    wg,
    local_sem,
    w_send,
    w_recv,
    x_send,
    x_recv,
    s_send,
    s_recv,
    right_send,
    left_send,
    z_recv,
):
    feats, blocks, _, depth = x_ref.shape
    shards_g = gat.shape[0]
    half = feats // 2
    g = lax.axis_index("graph")
    f = lax.axis_index("feat")
    mesh_id = pl.DeviceIdType.MESH
    sib = f + 1 - 2 * lax.rem(f, 2)

    def feat_at(j):
        return lax.rem(f + j, feats)

    def graph_at(j):
        return lax.rem(g + j, shards_g)

    def w_rows(s):
        return wg.at[pl.ds(pl.multiple_of(s * depth, depth), depth)]

    def remote(src, dst, send_sem, recv_sem, where):
        return pltpu.make_async_remote_copy(
            src_ref=src,
            dst_ref=dst,
            send_sem=send_sem,
            recv_sem=recv_sem,
            device_id=where,
            device_id_type=mesh_id,
        )

    def w_direct(j):
        to = sib if j == 0 else feat_at(2 * j)
        return remote(w_ref, w_rows(f), w_send.at[j], w_recv.at[f], {"feat": to})

    def w_relay(j):
        s = feat_at(2 * j)
        return remote(w_rows(s), w_rows(s), w_send.at[half + j], w_recv.at[s], {"feat": sib})

    def x_copy(j, c):
        to = feat_at(j)
        return remote(
            x_ref.at[to, c], xg.at[f, c], x_send.at[j, c], x_recv.at[f, c], {"feat": to}
        )

    def x_arrival(j, c):
        s = feat_at(j)
        return remote(x_ref.at[s, c], xg.at[s, c], x_send.at[j, c], x_recv.at[s, c], {"feat": s})

    def s_copy(j):
        to = graph_at(j)
        return remote(send_ref.at[to], sends.at[g], s_send.at[j], s_recv.at[g], {"graph": to})

    def s_arrival(j):
        s = graph_at(j)
        return remote(send_ref.at[s], sends.at[s], s_send.at[j], s_recv.at[s], {"graph": s})

    def z_right(o, c):
        return remote(
            gat.at[o, c], gat.at[o, c], right_send.at[o, c], z_recv.at[o, c], {"graph": g + 1}
        )

    def z_left(o, c):
        return remote(
            gat.at[o, c], gat.at[o, c], left_send.at[o, c], z_recv.at[o, c], {"graph": g - 1}
        )

    own = [
        pltpu.make_async_copy(w_ref, w_rows(f), local_sem.at[0]),
        pltpu.make_async_copy(x_ref.at[f], xg.at[f], local_sem.at[1]),
        pltpu.make_async_copy(send_ref.at[g], sends.at[g], local_sem.at[2]),
    ]
    for copy in own:
        copy.start()
    barrier = pltpu.get_barrier_semaphore()
    for j in range(1, feats):
        pl.semaphore_signal(barrier, inc=1, device_id={"feat": feat_at(j)}, device_id_type=mesh_id)
    for j in range(1, shards_g):
        pl.semaphore_signal(barrier, inc=1, device_id={"graph": graph_at(j)}, device_id_type=mesh_id)
    pl.semaphore_wait(barrier, feats + shards_g - 2)

    def send_x(c):
        for j in range(1, feats):
            x_copy(j, c).start()

    for j in range(half):
        w_direct(j).start()
    for c in range(min(AHEAD, blocks)):
        send_x(c)
    for j in range(1, shards_g):
        s_copy(j).start()
    for j in range(1, half):
        w_relay(j).wait_recv()
        w_relay(j).start()
    for copy in own:
        copy.wait()
    for j in range(half):
        s = lax.rem(sib + 2 * j, feats)
        remote(w_ref, w_rows(s), w_send.at[0], w_recv.at[s], {"feat": sib}).wait_recv()

    def forward(t):
        for d in range(1, shards_g):
            c = t - d
            inside = jnp.logical_and(c >= 0, c < blocks)

            @pl.when(inside & (g - d >= 0) & (g + 1 < shards_g))
            def _():
                z_right(g - d, c).wait_recv()
                z_right(g - d, c).start()

            @pl.when(inside & (g + d < shards_g) & (g >= 1))
            def _():
                z_left(g + d, c).wait_recv()
                z_left(g + d, c).start()

    def step(c, carry):
        @pl.when(c + AHEAD < blocks)
        def _():
            send_x(c + AHEAD)

        for j in range(1, feats):
            x_arrival(j, c).wait_recv()
        rows = jnp.concatenate([xg[s, c] for s in range(feats)], axis=1)
        gat[g, c] = jnp.dot(rows, wg[...], preferred_element_type=jnp.float32).astype(gat.dtype)

        @pl.when(g + 1 < shards_g)
        def _():
            z_right(g, c).start()

        @pl.when(g >= 1)
        def _():
            z_left(g, c).start()

        forward(c)
        return carry

    lax.fori_loop(0, blocks, step, 0)

    def tail(t, carry):
        forward(t)
        return carry

    lax.fori_loop(blocks, blocks + shards_g - 1, tail, 0)

    def finish(c, carry):
        for j in range(1, feats):
            x_copy(j, c).wait_send()

        @pl.when(g + 1 < shards_g)
        def _():
            z_right(g, c).wait_send()

        @pl.when(g >= 1)
        def _():
            z_left(g, c).wait_send()

        for d in range(1, shards_g):

            @pl.when((g - d >= 0) & (g + 1 < shards_g))
            def _():
                z_right(g - d, c).wait_send()

            @pl.when((g - d >= 0) & (g + 1 == shards_g))
            def _():
                z_left(g - d, c).wait_recv()

            @pl.when((g + d < shards_g) & (g >= 1))
            def _():
                z_left(g + d, c).wait_send()

            @pl.when((g + d < shards_g) & (g == 0))
            def _():
                z_right(g + d, c).wait_recv()

        return carry

    lax.fori_loop(0, blocks, finish, 0)
    for j in range(half):
        w_direct(j).wait_send()
    for j in range(1, half):
        w_relay(j).wait_send()
    for j in range(1, shards_g):
        s_copy(j).wait_send()
        s_arrival(j).wait_recv()


def exchange(x, w, send):
    feats, blocks, rows, depth = x.shape
    width = w.shape[1]
    graphs = send.shape[0]
    dma = pltpu.SemaphoreType.DMA
    anywhere = pl.BlockSpec(memory_space=pl.ANY)
    whole = pl.BlockSpec(memory_space=pltpu.VMEM)
    return pl.pallas_call(
        exchange_kernel,
        in_specs=[anywhere, anywhere, whole],
        out_specs=[whole, whole],
        out_shape=[
            jax.ShapeDtypeStruct((graphs, blocks, rows, width), jnp.bfloat16),
            jax.ShapeDtypeStruct(send.shape, jnp.int32),
        ],
        scratch_shapes=[
            pltpu.VMEM((feats, blocks, rows, depth), jnp.bfloat16),
            pltpu.VMEM((feats * depth, width), jnp.bfloat16),
            dma((3,)),
            dma((feats,)),
            dma((feats,)),
            dma((feats, blocks)),
            dma((feats, blocks)),
            dma((graphs,)),
            dma((graphs,)),
            dma((graphs, blocks)),
            dma((graphs, blocks)),
            dma((graphs, blocks)),
        ],
        compiler_params=pltpu.CompilerParams(
            collective_id=0, has_side_effects=True, vmem_limit_bytes=40 << 20
        ),
        name="exchange",
    )(x, w, send)


def attention_kernel(
    rels_ref,
    slots_ref,
    sends_ref,
    front_ref,
    relw_ref,
    atts_ref,
    attt_ref,
    mask_ref,
    out_ref,
    values,
    scores,
    tatt,
    target,
    stack,
    raws,
    bias,
    weights,
):
    graphs, blocks, rows, width = front_ref.shape
    cap = values.shape[0] // (relw_ref.shape[0] * graphs)
    slots = graphs * cap
    hw = width // HEADS
    relations = relw_ref.shape[0]
    lists = mask_ref.shape[1]
    b = pl.program_id(0)

    @pl.when(b == 0)
    def _():
        head_of = lax.broadcasted_iota(jnp.int32, (8, width), 1) // hw
        row_of = lax.broadcasted_iota(jnp.int32, (8, width), 0)
        for r in range(relations):
            hi, lo = split_bf16(atts_ref[r : r + 1, :] * LOG2E)
            parts = [
                jnp.where(head_of == row_of, part.astype(jnp.float32), 0.0)
                for part in (hi, lo)
            ]
            att = jnp.concatenate(parts, axis=0).astype(jnp.bfloat16)

            def one_sender(q, carry):
                taken = jnp.concatenate(
                    [front_ref[q, sends_ref[q, 0, c]] for c in range(cap)], axis=0
                )
                v = jnp.dot(taken, relw_ref[r], preferred_element_type=jnp.float32)
                v = v.astype(jnp.bfloat16)
                both = lax.dot_general(att, v, NT, preferred_element_type=jnp.float32)
                both = both[:8] + both[8:]
                for c in range(cap):
                    values[r * slots + q * cap + c] = v[c * rows : (c + 1) * rows]
                    scores[r * slots + q * cap + c] = both[:, c * rows : (c + 1) * rows]
                return carry

            lax.fori_loop(0, graphs, one_sender, 0)
            hi, lo = split_bf16(attt_ref[r : r + 1, :] * LOG2E)
            for n, part in enumerate((hi, lo)):
                tatt[n, r * rows : (r + 1) * rows, :] = jnp.broadcast_to(
                    part.astype(jnp.float32), (rows, width)
                ).astype(jnp.bfloat16)
        stack[:, :, hw:] = jnp.ones((HEADS, lists * rows, hw), jnp.bfloat16)

    mine = front_ref.at[lax.axis_index("graph"), b]
    index = []
    for k in range(lists):
        rel = rels_ref[b, k]
        index.append((rel, rel * slots + slots_ref[b, k]))
    for k in range(lists):
        v = values[index[k][1]]
        for h in range(HEADS):
            stack[h, k * rows : (k + 1) * rows, :hw] = v[:, h * hw : (h + 1) * hw]
        bias[k] = jnp.where(mask_ref[0, k] > 0, 0.0, -jnp.inf)
    for h in range(HEADS):
        cols = slice(h * hw, (h + 1) * hw)
        own = mine[:, cols]
        both = lax.dot_general(
            own, tatt[0, :, cols], NT, preferred_element_type=jnp.float32
        ) + lax.dot_general(own, tatt[1, :, cols], NT, preferred_element_type=jnp.float32)
        for r in range(relations):
            target[r] = both[:, r * rows : (r + 1) * rows]
        top = None
        for k in range(lists):
            rel, place = index[k]
            raw = (target[rel] + scores[place, h : h + 1, :]) + bias[k]
            raws[k] = raw
            top = raw if top is None else jnp.maximum(top, raw)
        top = jnp.max(top, axis=1, keepdims=True)
        top = jnp.broadcast_to(jnp.maximum(top, 0.2 * top), (rows, rows))
        for k in range(lists):
            raw = raws[k]
            prob = jnp.exp2(jnp.maximum(raw, 0.2 * raw) - top)
            weights[:, k * rows : (k + 1) * rows] = prob.astype(jnp.bfloat16)
        summed = jnp.dot(weights[...], stack[h], preferred_element_type=jnp.float32)
        mixed = summed[:, :hw] / summed[:, hw:] + own.astype(jnp.float32)
        out_ref[:, cols] = jnp.where(
            mixed > 0, mixed, jnp.exp(jnp.minimum(mixed, 0.0)) - 1.0
        ).astype(out_ref.dtype)


def attention(rels, slots, sends, front, cap, relw, atts, attt, mask):
    graphs, _, rows, width = front.shape
    count = graphs * cap
    blocks, lists = mask.shape[:2]
    relations = relw.shape[0]
    hw = width // HEADS
    smem = pl.BlockSpec(memory_space=pltpu.SMEM)
    whole = pl.BlockSpec(memory_space=pltpu.VMEM)
    return pl.pallas_call(
        attention_kernel,
        grid=(blocks,),
        in_specs=[
            smem,
            smem,
            smem,
            whole,
            whole,
            whole,
            whole,
            pl.BlockSpec((1, lists, rows, rows), lambda b: (b, 0, 0, 0)),
        ],
        out_specs=pl.BlockSpec((rows, width), lambda b: (b, 0)),
        out_shape=jax.ShapeDtypeStruct((blocks * rows, width), jnp.bfloat16),
        scratch_shapes=[
            pltpu.VMEM((relations * count, rows, width), jnp.bfloat16),
            pltpu.VMEM((relations * count, 8, rows), jnp.float32),
            pltpu.VMEM((2, relations * rows, width), jnp.bfloat16),
            pltpu.VMEM((relations, rows, rows), jnp.float32),
            pltpu.VMEM((HEADS, lists * rows, 2 * hw), jnp.bfloat16),
            pltpu.VMEM((lists, rows, rows), jnp.float32),
            pltpu.VMEM((lists, rows, rows), jnp.float32),
            pltpu.VMEM((rows, lists * rows), jnp.bfloat16),
        ],
        compiler_params=pltpu.CompilerParams(vmem_limit_bytes=56 << 20),
        name="attention",
    )(rels, slots, sends, front, relw, atts, attt, mask)


def shards(x, w, relw, atts, attt, mask, rels, send, slots):
    rows = mask.shape[-1]
    blocks = mask.shape[0]
    cap = send.shape[2]
    x = x.reshape(-1, blocks, rows, x.shape[1])
    tiles = jnp.pad(send[0][:, None, :], ((0, 0), (0, 7), (0, 128 - cap)))
    front, sends = exchange(x, w, tiles)
    return attention(rels, slots, sends, front, cap, relw, atts, attt, mask)


def solution(mesh):
    placed = (
        P("graph", "feat"),
        P("feat", None),
        P(),
        P(),
        P(),
        P(("graph", "feat"), None, None, None),
        P(("graph", "feat"), None),
        P(("graph", "feat"), None, None),
        P(("graph", "feat"), None),
    )
    return jax.shard_map(
        shards, mesh=mesh, in_specs=placed, out_specs=P(("graph", "feat"), None), check_vma=False
    )
```

```python
import math

import jax
import jax.numpy as jnp
from jax import lax
from jax.experimental import pallas as pl
from jax.experimental.pallas import tpu as pltpu
from jax.sharding import PartitionSpec as P

HEADS = 4
CHUNKS = 2
LOG2E = math.log2(math.e)
NT = (((1,), (1,)), ((), ()))


def split_bf16(x):
    hi = x.astype(jnp.bfloat16)
    lo = (x - hi.astype(jnp.float32)).astype(jnp.bfloat16)
    return hi, lo


def layer_kernel(
    send_ref,
    rels_ref,
    slots_ref,
    x_ref,
    w_ref,
    relw_ref,
    atts_ref,
    attt_ref,
    mask_ref,
    out_ref,
    xg,
    wg,
    hid,
    stage,
    front,
    values,
    scores,
    satt,
    tatt,
    target,
    stack,
    raws,
    weights,
    live,
    bias,
    local_sem,
    w_send,
    w_recv,
    x_send,
    x_recv,
    z_send,
    z_recv,
):
    feats, blocks, rows, depth = x_ref.shape
    graphs, cap = send_ref.shape
    width = w_ref.shape[1]
    relations = relw_ref.shape[0]
    lists = mask_ref.shape[1]
    slots = graphs * cap
    hw = width // HEADS
    half = feats // 2
    part = blocks // CHUNKS
    g = lax.axis_index("graph")
    f = lax.axis_index("feat")
    mesh_id = pl.DeviceIdType.MESH
    sib = f + 1 - 2 * lax.rem(f, 2)

    def feat_at(j):
        return lax.rem(f + j, feats)

    def graph_at(j):
        place, bit = 0, 1
        while bit < graphs:
            place = place + bit * ((g // bit + j // bit) % 2)
            bit *= 2
        return place

    def w_rows(s):
        return wg.at[pl.ds(pl.multiple_of(s * depth, depth), depth)]

    def remote(src, dst, send_sem, recv_sem, where):
        return pltpu.make_async_remote_copy(
            src_ref=src,
            dst_ref=dst,
            send_sem=send_sem,
            recv_sem=recv_sem,
            device_id=where,
            device_id_type=mesh_id,
        )

    def w_direct(j):
        to = sib if j == 0 else feat_at(2 * j)
        return remote(w_ref, w_rows(f), w_send.at[j], w_recv.at[f], {"feat": to})

    def w_relay(j):
        s = feat_at(2 * j)
        return remote(w_rows(s), w_rows(s), w_send.at[half + j], w_recv.at[s], {"feat": sib})

    def piece(c):
        return pl.ds(c * part, part)

    def x_copy(j, c):
        to = feat_at(j)
        return remote(
            x_ref.at[to, piece(c)],
            xg.at[f, piece(c)],
            x_send.at[j, c],
            x_recv.at[f, c],
            {"feat": to},
        )

    def x_arrival(j, c):
        s = feat_at(j)
        return remote(
            x_ref.at[s, piece(c)],
            xg.at[s, piece(c)],
            x_send.at[j, c],
            x_recv.at[s, c],
            {"feat": s},
        )

    def z_copy(j, c):
        to = graph_at(j)
        return remote(
            stage.at[j, c], front.at[g, c], z_send.at[j, c], z_recv.at[g, c], {"graph": to}
        )

    def z_arrival(j, c):
        q = graph_at(j)
        return remote(
            stage.at[j, c], front.at[q, c], z_send.at[j, c], z_recv.at[q, c], {"graph": q}
        )

    own = [
        pltpu.make_async_copy(w_ref, w_rows(f), local_sem.at[0]),
        pltpu.make_async_copy(x_ref.at[f], xg.at[f], local_sem.at[1]),
    ]
    masks = pltpu.make_async_copy(mask_ref, live, local_sem.at[2])
    for copy in own:
        copy.start()
    barrier = pltpu.get_barrier_semaphore()
    for j in range(1, feats):
        pl.semaphore_signal(barrier, inc=1, device_id={"feat": feat_at(j)}, device_id_type=mesh_id)
    for j in range(1, graphs):
        pl.semaphore_signal(barrier, inc=1, device_id={"graph": graph_at(j)}, device_id_type=mesh_id)
    pl.semaphore_wait(barrier, feats + graphs - 2)

    for j in range(half):
        w_direct(j).start()
    for c in range(CHUNKS):
        for j in range(1, feats):
            x_copy(j, c).start()
    masks.start()

    head_of = lax.broadcasted_iota(jnp.int32, (8, width), 1) // hw
    row_of = lax.broadcasted_iota(jnp.int32, (8, width), 0)
    for r in range(relations):
        parts = [
            jnp.where(head_of == row_of, half_att.astype(jnp.float32), 0.0)
            for half_att in split_bf16(atts_ref[r : r + 1, :] * LOG2E)
        ]
        satt[r] = jnp.concatenate(parts, axis=0).astype(jnp.bfloat16)
        for n, half_att in enumerate(split_bf16(attt_ref[r : r + 1, :] * LOG2E)):
            tatt[n, r * rows : (r + 1) * rows, :] = jnp.broadcast_to(
                half_att.astype(jnp.float32), (rows, width)
            ).astype(jnp.bfloat16)
    stack[:, :, hw:] = jnp.ones((HEADS, lists * rows, hw), jnp.bfloat16)

    for j in range(1, half):
        w_relay(j).wait_recv()
        w_relay(j).start()
    for copy in own:
        copy.wait()
    masks.wait()

    def make_bias(b, carry):
        bias[b] = jnp.where(live[b] > 0, 0.0, -jnp.inf)
        return carry

    lax.fori_loop(0, blocks, make_bias, 0)
    for j in range(half):
        s = lax.rem(sib + 2 * j, feats)
        remote(w_ref, w_rows(s), w_send.at[0], w_recv.at[s], {"feat": sib}).wait_recv()

    def project(c, carry):
        for j in range(1, feats):
            x_arrival(j, c).wait_recv()
        taken = jnp.concatenate(
            [xg[s, piece(c)].reshape(part * rows, depth) for s in range(feats)], axis=1
        )
        made = jnp.dot(taken, wg[...], preferred_element_type=jnp.float32)
        hid[piece(c)] = made.astype(hid.dtype).reshape(part, rows, width)
        return carry

    lax.fori_loop(0, CHUNKS, project, 0)

    def send_frontier(n, carry):
        j = graphs - 1 - n
        to = graph_at(j)
        for c in range(cap):
            stage[j, c] = hid[send_ref[to, c]]
            z_copy(j, c).start()
        return carry

    lax.fori_loop(0, graphs - 1, send_frontier, 0)
    for c in range(cap):
        front[g, c] = hid[send_ref[g, c]]

    def score_targets(c, carry):
        mine = hid[piece(c)].reshape(part * rows, width)
        for h in range(HEADS):
            cols = slice(h * hw, (h + 1) * hw)
            both = lax.dot_general(
                mine[:, cols], tatt[0, :, cols], NT, preferred_element_type=jnp.float32
            ) + lax.dot_general(
                mine[:, cols], tatt[1, :, cols], NT, preferred_element_type=jnp.float32
            )
            for r in range(relations):
                target[h, r, piece(c)] = both[:, r * rows : (r + 1) * rows].reshape(
                    part, rows, rows
                )
        return carry

    def transform(j):
        q = graph_at(j)
        taken = front[q].reshape(cap * rows, width)

        def relation(r, carry):
            v = jnp.dot(taken, relw_ref[r], preferred_element_type=jnp.float32)
            v = v.astype(jnp.bfloat16)
            both = lax.dot_general(satt[r], v, NT, preferred_element_type=jnp.float32)
            both = both[:8] + both[8:]
            for c in range(cap):
                values[r * slots + q * cap + c] = v[c * rows : (c + 1) * rows]
                scores[r * slots + q * cap + c] = both[:, c * rows : (c + 1) * rows]
            return carry

        lax.fori_loop(0, relations, relation, 0)

    transform(0)
    lax.fori_loop(0, CHUNKS, score_targets, 0)

    def receive(j, carry):
        for c in range(cap):
            z_arrival(j, c).wait_recv()
        transform(j)
        return carry

    lax.fori_loop(1, graphs, receive, 0)

    def attend(b, carry):
        index = []
        for k in range(lists):
            rel = rels_ref[b, k]
            index.append((rel, rel * slots + slots_ref[b, k]))
        for k in range(lists):
            v = values[index[k][1]]
            for h in range(HEADS):
                stack[h, k * rows : (k + 1) * rows, :hw] = v[:, h * hw : (h + 1) * hw]
        for h in range(HEADS):
            top = None
            for k in range(lists):
                rel, place = index[k]
                raw = (target[h, rel, b] + scores[place, h : h + 1, :]) + bias[b, k]
                raws[h, k] = raw
                top = raw if top is None else jnp.maximum(top, raw)
            top = jnp.max(top, axis=1, keepdims=True)
            top = jnp.broadcast_to(jnp.maximum(top, 0.2 * top), (rows, rows))
            for k in range(lists):
                raw = raws[h, k]
                prob = jnp.exp2(jnp.maximum(raw, 0.2 * raw) - top)
                weights[h, :, k * rows : (k + 1) * rows] = prob.astype(jnp.bfloat16)
        for h in range(HEADS):
            cols = slice(h * hw, (h + 1) * hw)
            summed = jnp.dot(weights[h], stack[h], preferred_element_type=jnp.float32)
            mixed = summed[:, :hw] / summed[:, hw:] + hid[b, :, cols].astype(jnp.float32)
            out_ref[b, :, cols] = jnp.where(
                mixed > 0, mixed, jnp.exp(jnp.minimum(mixed, 0.0)) - 1.0
            ).astype(out_ref.dtype)
        return carry

    lax.fori_loop(0, blocks, attend, 0)

    for c in range(CHUNKS):
        for j in range(1, feats):
            x_copy(j, c).wait_send()
    for j in range(half):
        w_direct(j).wait_send()
    for j in range(1, half):
        w_relay(j).wait_send()
    for j in range(1, graphs):
        for c in range(cap):
            z_copy(j, c).wait_send()


def layer(send, rels, slots, x, w, relw, atts, attt, mask):
    feats, blocks, rows, depth = x.shape
    width = w.shape[1]
    graphs, cap = send.shape
    lists = mask.shape[1]
    relations = relw.shape[0]
    count = relations * graphs * cap
    hw = width // HEADS
    dma = pltpu.SemaphoreType.DMA
    anywhere = pl.BlockSpec(memory_space=pl.ANY)
    whole = pl.BlockSpec(memory_space=pltpu.VMEM)
    smem = pl.BlockSpec(memory_space=pltpu.SMEM)
    bf16, f32 = jnp.bfloat16, jnp.float32
    return pl.pallas_call(
        layer_kernel,
        in_specs=[smem, smem, smem, anywhere, anywhere, whole, whole, whole, anywhere],
        out_specs=whole,
        out_shape=jax.ShapeDtypeStruct((blocks, rows, width), bf16),
        scratch_shapes=[
            pltpu.VMEM((feats, blocks, rows, depth), bf16),
            pltpu.VMEM((feats * depth, width), bf16),
            pltpu.VMEM((blocks, rows, width), bf16),
            pltpu.VMEM((graphs, cap, rows, width), bf16),
            pltpu.VMEM((graphs, cap, rows, width), bf16),
            pltpu.VMEM((count, rows, width), bf16),
            pltpu.VMEM((count, 8, rows), f32),
            pltpu.VMEM((relations, 16, width), bf16),
            pltpu.VMEM((2, relations * rows, width), bf16),
            pltpu.VMEM((HEADS, relations, blocks, rows, rows), f32),
            pltpu.VMEM((HEADS, lists * rows, 2 * hw), bf16),
            pltpu.VMEM((HEADS, lists, rows, rows), f32),
            pltpu.VMEM((HEADS, rows, lists * rows), bf16),
            pltpu.VMEM(mask.shape, jnp.int32),
            pltpu.VMEM(mask.shape, f32),
            dma((3,)),
            dma((feats,)),
            dma((feats,)),
            dma((feats, CHUNKS)),
            dma((feats, CHUNKS)),
            dma((graphs, cap)),
            dma((graphs, cap)),
        ],
        compiler_params=pltpu.CompilerParams(
            collective_id=0, has_side_effects=True, vmem_limit_bytes=58 << 20
        ),
        name="layer",
    )(send, rels, slots, x, w, relw, atts, attt, mask)


def shards(x, w, relw, atts, attt, mask, rels, send, slots):
    rows = mask.shape[-1]
    blocks = mask.shape[0]
    x = x.reshape(-1, blocks, rows, x.shape[1])
    out = layer(send[0], rels, slots, x, w, relw, atts, attt, mask)
    return out.reshape(blocks * rows, -1)


def solution(mesh):
    placed = (
        P("graph", "feat"),
        P("feat", None),
        P(),
        P(),
        P(),
        P(("graph", "feat"), None, None, None),
        P(("graph", "feat"), None),
        P(("graph", "feat"), None, None),
        P(("graph", "feat"), None),
    )
    return jax.shard_map(
        shards, mesh=mesh, in_specs=placed, out_specs=P(("graph", "feat"), None), check_vma=False
    )
```

```python
import math

import jax
import jax.numpy as jnp
from jax import lax
from jax.experimental import pallas as pl
from jax.experimental.pallas import tpu as pltpu
from jax.sharding import PartitionSpec as P

HEADS = 4
LOG2E = math.log2(math.e)
NT = (((1,), (1,)), ((), ()))


def split_bf16(x):
    hi = x.astype(jnp.bfloat16)
    lo = (x - hi.astype(jnp.float32)).astype(jnp.bfloat16)
    return hi, lo


def layer_kernel(
    send_ref,
    tiles_ref,
    rels_ref,
    slots_ref,
    x_ref,
    w_ref,
    relw_ref,
    atts_ref,
    attt_ref,
    mask_ref,
    out_ref,
    lists_got,
    lists_smem,
    spot,
    xin,
    xst,
    xg,
    wg,
    hid,
    stage,
    front,
    values,
    scores,
    satt,
    tatt,
    target,
    stack,
    raws,
    weights,
    live,
    bias,
    local_sem,
    l_send,
    l_recv,
    w_send,
    w_recv,
    x_send,
    x_recv,
    z_send,
    z_recv,
):
    feats, blocks, rows, depth = x_ref.shape
    graphs, cap = send_ref.shape
    width = w_ref.shape[1]
    relations = relw_ref.shape[0]
    lists = mask_ref.shape[1]
    slots = graphs * cap
    hw = width // HEADS
    parts = ((0, cap), (cap, blocks - cap))
    g = lax.axis_index("graph")
    f = lax.axis_index("feat")
    mesh_id = pl.DeviceIdType.MESH
    parity = lax.rem(f, 2)

    def flip(index, bits, size):
        place, bit = 0, 1
        while bit < size:
            place = place + bit * ((index // bit + bits // bit) % 2)
            bit *= 2
        return place

    if feats == 8:
        even, odd = (2, 4, 6, 3, 5, 7, 1), (4, 2, 7, 5, 3, 6, 1)
    else:
        even = odd = tuple(range(1, feats))
    pairs = tuple(m for m in range(2, feats, 2))
    turns = tuple(pairs[1:2] + pairs[:1] + pairs[2:])

    def feat_at(n):
        return flip(f, even[n] + parity * (odd[n] - even[n]), feats)

    def same_core(n):
        return flip(f, pairs[n] + parity * (turns[n] - pairs[n]), feats)

    sib = f + 1 - 2 * parity
    others = range(feats - 1)
    chips = range(len(pairs))
    inner = jnp.logical_and(g > 0, g < graphs - 1)

    def graph_at(j):
        return flip(g, j, graphs)

    def order(n):
        return graphs - 1 - n + jnp.where(inner, 1 if n else 2 - graphs, 0)

    def w_rows(s):
        return wg.at[pl.ds(pl.multiple_of(s * depth, depth), depth)]

    def remote(src, dst, send_sem, recv_sem, where):
        return pltpu.make_async_remote_copy(
            src_ref=src,
            dst_ref=dst,
            send_sem=send_sem,
            recv_sem=recv_sem,
            device_id=where,
            device_id_type=mesh_id,
        )

    def w_direct(n):
        to = same_core(n) if n < len(pairs) else sib
        return remote(w_ref, w_rows(f), w_send.at[n], w_recv.at[f], {"feat": to})

    def w_relay(n):
        s = same_core(n)
        return remote(w_rows(s), w_rows(s), w_send.at[feats + n], w_recv.at[s], {"feat": sib})

    def piece(c):
        return pl.ds(*parts[c])

    def x_copy(n, c):
        to = feat_at(n)
        return remote(
            xst.at[to, piece(c)],
            xg.at[f, piece(c)],
            x_send.at[n, c],
            x_recv.at[f, c],
            {"feat": to},
        )

    def x_arrival(n, c):
        s = feat_at(n)
        return remote(
            xst.at[s, piece(c)],
            xg.at[s, piece(c)],
            x_send.at[n, c],
            x_recv.at[s, c],
            {"feat": s},
        )

    first = graph_at(order(0))

    def l_copy(n):
        to = feat_at(n)
        return remote(
            tiles_ref.at[first], lists_got.at[f], l_send.at[n], l_recv.at[f], {"feat": to}
        )

    def l_arrival(n):
        s = feat_at(n)
        return remote(
            tiles_ref.at[first], lists_got.at[s], l_send.at[n], l_recv.at[s], {"feat": s}
        )

    def z_first(c):
        j = order(0)
        return remote(
            hid.at[c], front.at[g, c], z_send.at[j, c], z_recv.at[g, c], {"graph": first}
        )

    def z_copy(j, c):
        to = graph_at(j)
        return remote(
            stage.at[j, c], front.at[g, c], z_send.at[j, c], z_recv.at[g, c], {"graph": to}
        )

    def z_arrival(j, c):
        q = graph_at(j)
        return remote(
            stage.at[j, c], front.at[q, c], z_send.at[j, c], z_recv.at[q, c], {"graph": q}
        )

    own = [
        pltpu.make_async_copy(w_ref, w_rows(f), local_sem.at[0]),
        pltpu.make_async_copy(x_ref, xin, local_sem.at[1]),
        pltpu.make_async_copy(tiles_ref.at[first], lists_got.at[f], local_sem.at[2]),
    ]
    masks = pltpu.make_async_copy(mask_ref, live, local_sem.at[3])
    for copy in own:
        copy.start()
    barrier = pltpu.get_barrier_semaphore()
    for n in others:
        pl.semaphore_signal(barrier, inc=1, device_id={"feat": feat_at(n)}, device_id_type=mesh_id)
    for j in range(1, graphs):
        pl.semaphore_signal(barrier, inc=1, device_id={"graph": graph_at(j)}, device_id_type=mesh_id)
    pl.semaphore_wait(barrier, feats + graphs - 2)

    for n in others:
        l_copy(n).start()
    for n in range(len(pairs) + 1):
        w_direct(n).start()
    for copy in own:
        copy.wait()
    for n in others:
        l_arrival(n).wait_recv()
    to_smem = pltpu.make_async_copy(lists_got, lists_smem, local_sem.at[4])
    to_smem.start()
    to_smem.wait()

    def unlisted(s, block):
        used = 0
        for c in range(cap):
            used = used + jnp.where(lists_smem[s, 0, c] == block, 1, 0)
        return 1 - jnp.minimum(used, 1)

    def fill(s, c):
        if c == 0:
            for t in range(cap):
                xst[s, t] = xin[s, lists_smem[s, 0, t]]
        else:
            free = [unlisted(s, block) for block in range(blocks)]
            for t in range(blocks - cap):
                found, seen = 0, 0
                for block in range(blocks):
                    hit = jnp.where(seen == t, free[block], 0)
                    found = found + hit * block
                    seen = seen + free[block]
                xst[s, cap + t] = xin[s, jnp.minimum(found, blocks - 1)]

    for n in others:
        fill(feat_at(n), 0)
        x_copy(n, 0).start()
    for n in chips:
        w_relay(n).wait_recv()
        w_relay(n).start()
    for n in others:
        fill(feat_at(n), 1)
        x_copy(n, 1).start()
    for c in range(2):
        fill(f, c)
    seen = 0
    for block in range(blocks):
        place = 0
        for c in range(cap):
            place = place + jnp.where(lists_smem[f, 0, c] == block, c, 0)
        free = unlisted(f, block)
        spot[block] = jnp.minimum(place + free * (cap + seen), blocks - 1)
        seen = seen + free
    masks.start()

    head_of = lax.broadcasted_iota(jnp.int32, (8, width), 1) // hw
    row_of = lax.broadcasted_iota(jnp.int32, (8, width), 0)
    for r in range(relations):
        halves = [
            jnp.where(head_of == row_of, half_att.astype(jnp.float32), 0.0)
            for half_att in split_bf16(atts_ref[r : r + 1, :] * LOG2E)
        ]
        satt[r] = jnp.concatenate(halves, axis=0).astype(jnp.bfloat16)
        for n, half_att in enumerate(split_bf16(attt_ref[r : r + 1, :] * LOG2E)):
            tatt[n, r * rows : (r + 1) * rows, :] = jnp.broadcast_to(
                half_att.astype(jnp.float32), (rows, width)
            ).astype(jnp.bfloat16)
    stack[:, :, hw:] = jnp.ones((HEADS, lists * rows, hw), jnp.bfloat16)

    masks.wait()

    def make_bias(b, carry):
        bias[b] = jnp.where(live[b] > 0, 0.0, -jnp.inf)
        return carry

    lax.fori_loop(0, blocks, make_bias, 0)
    for n in range(len(pairs) + 1):
        s = flip(sib, 2 * n, feats)
        remote(w_ref, w_rows(s), w_send.at[0], w_recv.at[s], {"feat": sib}).wait_recv()

    def project(c):
        size = parts[c][1]
        for n in others:
            x_arrival(n, c).wait_recv()
        xg[f, piece(c)] = xst[f, piece(c)]
        taken = jnp.concatenate(
            [xg[s, piece(c)].reshape(size * rows, depth) for s in range(feats)], axis=1
        )
        made = jnp.dot(taken, wg[...], preferred_element_type=jnp.float32)
        hid[piece(c)] = made.astype(hid.dtype).reshape(size, rows, width)

    project(0)
    for c in range(cap):
        z_first(c).start()
    project(1)
    for n in range(1, graphs - 1):
        j = order(n)
        to = graph_at(j)
        for c in range(cap):
            stage[j, c] = hid[spot[send_ref[to, c]]]
            z_copy(j, c).start()
    for c in range(cap):
        front[g, c] = hid[spot[send_ref[g, c]]]

    def score_targets(c):
        size = parts[c][1]
        mine = hid[piece(c)].reshape(size * rows, width)
        for h in range(HEADS):
            cols = slice(h * hw, (h + 1) * hw)
            both = lax.dot_general(
                mine[:, cols], tatt[0, :, cols], NT, preferred_element_type=jnp.float32
            ) + lax.dot_general(
                mine[:, cols], tatt[1, :, cols], NT, preferred_element_type=jnp.float32
            )
            for r in range(relations):
                target[h, r, piece(c)] = both[:, r * rows : (r + 1) * rows].reshape(
                    size, rows, rows
                )

    def transform(j):
        q = graph_at(j)
        taken = front[q].reshape(cap * rows, width)

        def relation(r, carry):
            v = jnp.dot(taken, relw_ref[r], preferred_element_type=jnp.float32)
            v = v.astype(jnp.bfloat16)
            both = lax.dot_general(satt[r], v, NT, preferred_element_type=jnp.float32)
            both = both[:8] + both[8:]
            for c in range(cap):
                values[r * slots + q * cap + c] = v[c * rows : (c + 1) * rows]
                scores[r * slots + q * cap + c] = both[:, c * rows : (c + 1) * rows]
            return carry

        lax.fori_loop(0, relations, relation, 0)

    transform(0)
    for c in range(2):
        score_targets(c)

    def receive(j, carry):
        for c in range(cap):
            z_arrival(j, c).wait_recv()
        transform(j)
        return carry

    lax.fori_loop(1, graphs, receive, 0)

    def attend(b, carry):
        at = spot[b]
        index = []
        for k in range(lists):
            rel = rels_ref[b, k]
            index.append((rel, rel * slots + slots_ref[b, k]))
        for k in range(lists):
            v = values[index[k][1]]
            for h in range(HEADS):
                stack[h, k * rows : (k + 1) * rows, :hw] = v[:, h * hw : (h + 1) * hw]
        for h in range(HEADS):
            top = None
            for k in range(lists):
                rel, place = index[k]
                raw = (target[h, rel, at] + scores[place, h : h + 1, :]) + bias[b, k]
                raws[h, k] = raw
                top = raw if top is None else jnp.maximum(top, raw)
            top = jnp.max(top, axis=1, keepdims=True)
            top = jnp.broadcast_to(jnp.maximum(top, 0.2 * top), (rows, rows))
            for k in range(lists):
                raw = raws[h, k]
                prob = jnp.exp2(jnp.maximum(raw, 0.2 * raw) - top)
                weights[h, :, k * rows : (k + 1) * rows] = prob.astype(jnp.bfloat16)
        for h in range(HEADS):
            cols = slice(h * hw, (h + 1) * hw)
            summed = jnp.dot(weights[h], stack[h], preferred_element_type=jnp.float32)
            mixed = summed[:, :hw] / summed[:, hw:] + hid[at, :, cols].astype(jnp.float32)
            out_ref[b, :, cols] = jnp.where(
                mixed > 0, mixed, jnp.exp(jnp.minimum(mixed, 0.0)) - 1.0
            ).astype(out_ref.dtype)
        return carry

    lax.fori_loop(0, blocks, attend, 0)

    for n in others:
        l_copy(n).wait_send()
        for c in range(2):
            x_copy(n, c).wait_send()
    for n in range(len(pairs) + 1):
        w_direct(n).wait_send()
    for n in chips:
        w_relay(n).wait_send()
    for j in range(1, graphs):
        for c in range(cap):
            z_copy(j, c).wait_send()


def layer(send, tiles, rels, slots, x, w, relw, atts, attt, mask):
    feats, blocks, rows, depth = x.shape
    width = w.shape[1]
    graphs, cap = send.shape
    lists = mask.shape[1]
    relations = relw.shape[0]
    count = relations * graphs * cap
    hw = width // HEADS
    dma = pltpu.SemaphoreType.DMA
    anywhere = pl.BlockSpec(memory_space=pl.ANY)
    whole = pl.BlockSpec(memory_space=pltpu.VMEM)
    smem = pl.BlockSpec(memory_space=pltpu.SMEM)
    bf16, f32 = jnp.bfloat16, jnp.float32
    return pl.pallas_call(
        layer_kernel,
        in_specs=[smem, whole, smem, smem, anywhere, anywhere, whole, whole, whole, anywhere],
        out_specs=whole,
        out_shape=jax.ShapeDtypeStruct((blocks, rows, width), bf16),
        scratch_shapes=[
            pltpu.VMEM((feats,) + tiles.shape[1:], jnp.int32),
            pltpu.SMEM((feats,) + tiles.shape[1:], jnp.int32),
            pltpu.SMEM((blocks,), jnp.int32),
            pltpu.VMEM((feats, blocks, rows, depth), bf16),
            pltpu.VMEM((feats, blocks, rows, depth), bf16),
            pltpu.VMEM((feats, blocks, rows, depth), bf16),
            pltpu.VMEM((feats * depth, width), bf16),
            pltpu.VMEM((blocks, rows, width), bf16),
            pltpu.VMEM((graphs, cap, rows, width), bf16),
            pltpu.VMEM((graphs, cap, rows, width), bf16),
            pltpu.VMEM((count, rows, width), bf16),
            pltpu.VMEM((count, 8, rows), f32),
            pltpu.VMEM((relations, 16, width), bf16),
            pltpu.VMEM((2, relations * rows, width), bf16),
            pltpu.VMEM((HEADS, relations, blocks, rows, rows), f32),
            pltpu.VMEM((HEADS, lists * rows, 2 * hw), bf16),
            pltpu.VMEM((HEADS, lists, rows, rows), f32),
            pltpu.VMEM((HEADS, rows, lists * rows), bf16),
            pltpu.VMEM(mask.shape, jnp.int32),
            pltpu.VMEM(mask.shape, f32),
            dma((5,)),
            dma((feats,)),
            dma((feats,)),
            dma((2 * feats,)),
            dma((feats,)),
            dma((feats, 2)),
            dma((feats, 2)),
            dma((graphs, cap)),
            dma((graphs, cap)),
        ],
        compiler_params=pltpu.CompilerParams(
            collective_id=0, has_side_effects=True, vmem_limit_bytes=58 << 20
        ),
        name="layer",
    )(send, tiles, rels, slots, x, w, relw, atts, attt, mask)


def shards(x, w, relw, atts, attt, mask, rels, send, slots):
    rows = mask.shape[-1]
    blocks = mask.shape[0]
    x = x.reshape(-1, blocks, rows, x.shape[1])
    cap = send.shape[2]
    tiles = jnp.pad(send[0][:, None, :], ((0, 0), (0, 7), (0, 128 - cap)))
    out = layer(send[0], tiles, rels, slots, x, w, relw, atts, attt, mask)
    return out.reshape(blocks * rows, -1)


def solution(mesh):
    placed = (
        P("graph", "feat"),
        P("feat", None),
        P(),
        P(),
        P(),
        P(("graph", "feat"), None, None, None),
        P(("graph", "feat"), None),
        P(("graph", "feat"), None, None),
        P(("graph", "feat"), None),
    )
    return jax.shard_map(
        shards, mesh=mesh, in_specs=placed, out_specs=P(("graph", "feat"), None), check_vma=False
    )
```

```python
import math

import jax
import jax.numpy as jnp
from jax import lax
from jax.experimental import pallas as pl
from jax.experimental.pallas import tpu as pltpu
from jax.sharding import PartitionSpec as P

HEADS = 4
LOG2E = math.log2(math.e)
NT = (((1,), (1,)), ((), ()))


def split_bf16(x):
    hi = x.astype(jnp.bfloat16)
    lo = (x - hi.astype(jnp.float32)).astype(jnp.bfloat16)
    return hi, lo


def layer_kernel(
    send_ref,
    rels_ref,
    slots_ref,
    x_ref,
    w_ref,
    relw_ref,
    atts_ref,
    attt_ref,
    mask_ref,
    out_ref,
    tile,
    lists_got,
    lists_smem,
    spot,
    xin,
    xst,
    xg,
    wg,
    hid,
    stage,
    front,
    values,
    scores,
    satt,
    tatt,
    target,
    stack0,
    stack1,
    raws0,
    raws1,
    weights0,
    weights1,
    live,
    bias,
    local_sem,
    l_send,
    l_recv,
    w_send,
    w_recv,
    x_send,
    x_recv,
    z_send,
    z_recv,
):
    feats, blocks, rows, depth = x_ref.shape
    graphs, cap = send_ref.shape
    width = w_ref.shape[1]
    relations = relw_ref.shape[0]
    lists = mask_ref.shape[1]
    slots = graphs * cap
    hw = width // HEADS
    stack, raws, weights = (stack0, stack1), (raws0, raws1), (weights0, weights1)
    parts = ((0, cap), (cap, blocks - cap))
    g = lax.axis_index("graph")
    f = lax.axis_index("feat")
    mesh_id = pl.DeviceIdType.MESH
    parity = lax.rem(f, 2)

    def flip(index, bits, size):
        place, bit = 0, 1
        while bit < size:
            place = place + bit * ((index // bit + bits // bit) % 2)
            bit *= 2
        return place

    if feats == 8:
        even, odd = (2, 4, 6, 3, 5, 7, 1), (4, 2, 7, 5, 3, 6, 1)
    else:
        even = odd = tuple(range(1, feats))
    pairs = tuple(m for m in range(2, feats, 2))
    turns = tuple(pairs[1:2] + pairs[:1] + pairs[2:])

    def feat_at(n):
        return flip(f, even[n] + parity * (odd[n] - even[n]), feats)

    def same_core(n):
        return flip(f, pairs[n] + parity * (turns[n] - pairs[n]), feats)

    sib = f + 1 - 2 * parity
    others = range(feats - 1)
    chips = range(len(pairs))
    inner = jnp.logical_and(g > 0, g < graphs - 1)

    def graph_at(j):
        return flip(g, j, graphs)

    def order(n):
        return graphs - 1 - n + jnp.where(inner, 1 if n else 2 - graphs, 0)

    def w_rows(s):
        return wg.at[pl.ds(pl.multiple_of(s * depth, depth), depth)]

    def remote(src, dst, send_sem, recv_sem, where):
        return pltpu.make_async_remote_copy(
            src_ref=src,
            dst_ref=dst,
            send_sem=send_sem,
            recv_sem=recv_sem,
            device_id=where,
            device_id_type=mesh_id,
        )

    def w_direct(n):
        to = same_core(n) if n < len(pairs) else sib
        return remote(w_ref, w_rows(f), w_send.at[n], w_recv.at[f], {"feat": to})

    def w_relay(n):
        s = same_core(n)
        return remote(w_rows(s), w_rows(s), w_send.at[feats + n], w_recv.at[s], {"feat": sib})

    def piece(c):
        return pl.ds(*parts[c])

    def x_copy(n, c):
        to = feat_at(n)
        return remote(
            xst.at[to, piece(c)],
            xg.at[f, piece(c)],
            x_send.at[n, c],
            x_recv.at[f, c],
            {"feat": to},
        )

    def x_arrival(n, c):
        s = feat_at(n)
        return remote(
            xst.at[s, piece(c)],
            xg.at[s, piece(c)],
            x_send.at[n, c],
            x_recv.at[s, c],
            {"feat": s},
        )

    first = graph_at(order(0))

    def l_copy(n):
        to = feat_at(n)
        return remote(
            tile, lists_got.at[f], l_send.at[n], l_recv.at[f], {"feat": to}
        )

    def l_arrival(n):
        s = feat_at(n)
        return remote(
            tile, lists_got.at[s], l_send.at[n], l_recv.at[s], {"feat": s}
        )

    def z_first(c):
        j = order(0)
        return remote(
            hid.at[c], front.at[g, c], z_send.at[j, c], z_recv.at[g, c], {"graph": first}
        )

    def z_copy(j, c):
        to = graph_at(j)
        return remote(
            stage.at[j, c], front.at[g, c], z_send.at[j, c], z_recv.at[g, c], {"graph": to}
        )

    def z_arrival(j, c):
        q = graph_at(j)
        return remote(
            stage.at[j, c], front.at[q, c], z_send.at[j, c], z_recv.at[q, c], {"graph": q}
        )

    own = [
        pltpu.make_async_copy(w_ref, w_rows(f), local_sem.at[0]),
        pltpu.make_async_copy(x_ref, xin, local_sem.at[1]),
    ]
    lane = lax.broadcasted_iota(jnp.int32, tile.shape, 1)
    listed = jnp.zeros(tile.shape, jnp.int32)
    for c in range(cap):
        listed = jnp.where(lane == c, send_ref[first, c], listed)
    tile[...] = listed
    lists_got[f] = listed
    masks = pltpu.make_async_copy(mask_ref, live, local_sem.at[3])
    for copy in own:
        copy.start()
    barrier = pltpu.get_barrier_semaphore()
    for n in others:
        pl.semaphore_signal(barrier, inc=1, device_id={"feat": feat_at(n)}, device_id_type=mesh_id)
    for j in range(1, graphs):
        pl.semaphore_signal(barrier, inc=1, device_id={"graph": graph_at(j)}, device_id_type=mesh_id)
    pl.semaphore_wait(barrier, feats + graphs - 2)

    for n in others:
        l_copy(n).start()
    for n in range(len(pairs) + 1):
        w_direct(n).start()
    for copy in own:
        copy.wait()
    for n in others:
        l_arrival(n).wait_recv()
    to_smem = pltpu.make_async_copy(lists_got, lists_smem, local_sem.at[4])
    to_smem.start()
    to_smem.wait()

    def unlisted(s, block):
        used = 0
        for c in range(cap):
            used = used + jnp.where(lists_smem[s, 0, c] == block, 1, 0)
        return 1 - jnp.minimum(used, 1)

    def fill(s, c):
        if c == 0:
            for t in range(cap):
                xst[s, t] = xin[s, lists_smem[s, 0, t]]
        else:
            free = [unlisted(s, block) for block in range(blocks)]
            for t in range(blocks - cap):
                found, seen = 0, 0
                for block in range(blocks):
                    hit = jnp.where(seen == t, free[block], 0)
                    found = found + hit * block
                    seen = seen + free[block]
                xst[s, cap + t] = xin[s, jnp.minimum(found, blocks - 1)]

    for n in others:
        fill(feat_at(n), 0)
        x_copy(n, 0).start()
    for n in chips:
        w_relay(n).wait_recv()
        w_relay(n).start()
    for n in others:
        fill(feat_at(n), 1)
        x_copy(n, 1).start()
    for c in range(2):
        fill(f, c)
    seen = 0
    for block in range(blocks):
        place = 0
        for c in range(cap):
            place = place + jnp.where(lists_smem[f, 0, c] == block, c, 0)
        free = unlisted(f, block)
        spot[block] = jnp.minimum(place + free * (cap + seen), blocks - 1)
        seen = seen + free
    masks.start()

    head_of = lax.broadcasted_iota(jnp.int32, (8, width), 1) // hw
    row_of = lax.broadcasted_iota(jnp.int32, (8, width), 0)
    for r in range(relations):
        halves = [
            jnp.where(head_of == row_of, half_att.astype(jnp.float32), 0.0)
            for half_att in split_bf16(atts_ref[r : r + 1, :] * LOG2E)
        ]
        satt[r] = jnp.concatenate(halves, axis=0).astype(jnp.bfloat16)
        for n, half_att in enumerate(split_bf16(attt_ref[r : r + 1, :] * LOG2E)):
            tatt[n, r * rows : (r + 1) * rows, :] = jnp.broadcast_to(
                half_att.astype(jnp.float32), (rows, width)
            ).astype(jnp.bfloat16)

    masks.wait()

    def make_bias(b, carry):
        bias[b] = jnp.where(live[b] > 0, 0.0, -jnp.inf)
        return carry

    lax.fori_loop(0, blocks, make_bias, 0)
    for n in range(len(pairs) + 1):
        s = flip(sib, 2 * n, feats)
        remote(w_ref, w_rows(s), w_send.at[0], w_recv.at[s], {"feat": sib}).wait_recv()

    def project(c):
        size = parts[c][1]
        for n in others:
            x_arrival(n, c).wait_recv()
        xg[f, piece(c)] = xst[f, piece(c)]
        taken = jnp.concatenate(
            [xg[s, piece(c)].reshape(size * rows, depth) for s in range(feats)], axis=1
        )
        made = jnp.dot(taken, wg[...], preferred_element_type=jnp.float32)
        hid[piece(c)] = made.astype(hid.dtype).reshape(size, rows, width)

    project(0)
    for c in range(cap):
        z_first(c).start()
    project(1)
    for n in range(1, graphs - 1):
        j = order(n)
        to = graph_at(j)
        for c in range(cap):
            stage[j, c] = hid[spot[send_ref[to, c]]]
            z_copy(j, c).start()
    for c in range(cap):
        front[g, c] = hid[spot[send_ref[g, c]]]

    def score_targets(c):
        size = parts[c][1]
        mine = hid[piece(c)].reshape(size * rows, width)
        for h in range(HEADS):
            cols = slice(h * hw, (h + 1) * hw)
            both = lax.dot_general(
                mine[:, cols], tatt[0, :, cols], NT, preferred_element_type=jnp.float32
            ) + lax.dot_general(
                mine[:, cols], tatt[1, :, cols], NT, preferred_element_type=jnp.float32
            )
            for r in range(relations):
                target[h, r, piece(c)] = both[:, r * rows : (r + 1) * rows].reshape(
                    size, rows, rows
                )

    def transform(j):
        q = graph_at(j)
        taken = front[q].reshape(cap * rows, width)

        def relation(r, carry):
            v = jnp.dot(taken, relw_ref[r], preferred_element_type=jnp.float32)
            v = v.astype(jnp.bfloat16)
            both = lax.dot_general(satt[r], v, NT, preferred_element_type=jnp.float32)
            both = both[:8] + both[8:]
            for c in range(cap):
                values[r * slots + q * cap + c] = v[c * rows : (c + 1) * rows]
                scores[r * slots + q * cap + c] = both[:, c * rows : (c + 1) * rows]
            return carry

        lax.fori_loop(0, relations, relation, 0)

    transform(0)
    for c in range(2):
        score_targets(c)

    def receive(j, carry):
        for c in range(cap):
            z_arrival(j, c).wait_recv()
        transform(j)
        return carry

    lax.fori_loop(1, graphs, receive, 0)

    def attend(pair, carry):
        for u in range(2):
            attend_one(2 * pair + u, stack[u], raws[u], weights[u])
        return carry

    def attend_one(b, stacked, raw_buf, weight_buf):
        at = spot[b]
        index = []
        for k in range(lists):
            rel = rels_ref[b, k]
            index.append((rel, rel * slots + slots_ref[b, k]))
        for k in range(lists):
            stacked[k * rows : (k + 1) * rows, :] = values[index[k][1]]
        for m in range(HEADS // 2):
            totals = []
            for h in (2 * m, 2 * m + 1):
                top = None
                for k in range(lists):
                    rel, place = index[k]
                    raw = (target[h, rel, at] + scores[place, h : h + 1, :]) + bias[b, k]
                    raw_buf[h, k] = raw
                    top = raw if top is None else jnp.maximum(top, raw)
                top = jnp.max(top, axis=1, keepdims=True)
                top = jnp.broadcast_to(jnp.maximum(top, 0.2 * top), (rows, rows))
                total = None
                for k in range(lists):
                    raw = raw_buf[h, k]
                    prob = jnp.exp2(jnp.maximum(raw, 0.2 * raw) - top)
                    total = prob if total is None else total + prob
                    weight_buf[h * rows : (h + 1) * rows, k * rows : (k + 1) * rows] = (
                        prob.astype(jnp.bfloat16)
                    )
                totals.append(jnp.sum(total, axis=1, keepdims=True))
            both = jnp.dot(
                weight_buf[2 * m * rows : (2 * m + 2) * rows, :],
                stacked[:, 2 * m * hw : (2 * m + 2) * hw],
                preferred_element_type=jnp.float32,
            )
            for n in range(2):
                cols = slice((2 * m + n) * hw, (2 * m + n + 1) * hw)
                summed = both[n * rows : (n + 1) * rows, n * hw : (n + 1) * hw]
                mixed = summed * (1.0 / totals[n]) + hid[at, :, cols].astype(jnp.float32)
                out_ref[b, :, cols] = jnp.where(
                    mixed > 0, mixed, jnp.exp(jnp.minimum(mixed, 0.0)) - 1.0
                ).astype(out_ref.dtype)

    lax.fori_loop(0, blocks // 2, attend, 0)

    for n in others:
        l_copy(n).wait_send()
        for c in range(2):
            x_copy(n, c).wait_send()
    for n in range(len(pairs) + 1):
        w_direct(n).wait_send()
    for n in chips:
        w_relay(n).wait_send()
    for j in range(1, graphs):
        for c in range(cap):
            z_copy(j, c).wait_send()


def layer(send, rels, slots, x, w, relw, atts, attt, mask):
    feats, blocks, rows, depth = x.shape
    width = w.shape[1]
    graphs, cap = send.shape
    lists = mask.shape[1]
    relations = relw.shape[0]
    count = relations * graphs * cap
    hw = width // HEADS
    dma = pltpu.SemaphoreType.DMA
    anywhere = pl.BlockSpec(memory_space=pl.ANY)
    whole = pl.BlockSpec(memory_space=pltpu.VMEM)
    smem = pl.BlockSpec(memory_space=pltpu.SMEM)
    bf16, f32 = jnp.bfloat16, jnp.float32
    return pl.pallas_call(
        layer_kernel,
        in_specs=[smem, smem, smem, anywhere, anywhere, whole, whole, whole, anywhere],
        out_specs=whole,
        out_shape=jax.ShapeDtypeStruct((blocks, rows, width), bf16),
        scratch_shapes=[
            pltpu.VMEM((8, 128), jnp.int32),
            pltpu.VMEM((feats, 8, 128), jnp.int32),
            pltpu.SMEM((feats, 8, 128), jnp.int32),
            pltpu.SMEM((blocks,), jnp.int32),
            pltpu.VMEM((feats, blocks, rows, depth), bf16),
            pltpu.VMEM((feats, blocks, rows, depth), bf16),
            pltpu.VMEM((feats, blocks, rows, depth), bf16),
            pltpu.VMEM((feats * depth, width), bf16),
            pltpu.VMEM((blocks, rows, width), bf16),
            pltpu.VMEM((graphs, cap, rows, width), bf16),
            pltpu.VMEM((graphs, cap, rows, width), bf16),
            pltpu.VMEM((count, rows, width), bf16),
            pltpu.VMEM((count, 8, rows), f32),
            pltpu.VMEM((relations, 16, width), bf16),
            pltpu.VMEM((2, relations * rows, width), bf16),
            pltpu.VMEM((HEADS, relations, blocks, rows, rows), f32),
            pltpu.VMEM((lists * rows, width), bf16),
            pltpu.VMEM((lists * rows, width), bf16),
            pltpu.VMEM((HEADS, lists, rows, rows), f32),
            pltpu.VMEM((HEADS, lists, rows, rows), f32),
            pltpu.VMEM((HEADS * rows, lists * rows), bf16),
            pltpu.VMEM((HEADS * rows, lists * rows), bf16),
            pltpu.VMEM(mask.shape, jnp.int32),
            pltpu.VMEM(mask.shape, f32),
            dma((5,)),
            dma((feats,)),
            dma((feats,)),
            dma((2 * feats,)),
            dma((feats,)),
            dma((feats, 2)),
            dma((feats, 2)),
            dma((graphs, cap)),
            dma((graphs, cap)),
        ],
        compiler_params=pltpu.CompilerParams(
            collective_id=0, has_side_effects=True, vmem_limit_bytes=58 << 20
        ),
        name="layer",
    )(send, rels, slots, x, w, relw, atts, attt, mask)


def shards(x, w, relw, atts, attt, mask, rels, send, slots):
    rows = mask.shape[-1]
    blocks = mask.shape[0]
    x = x.reshape(-1, blocks, rows, x.shape[1])
    out = layer(send[0], rels, slots, x, w, relw, atts, attt, mask)
    return out.reshape(blocks * rows, -1)


def solution(mesh):
    placed = (
        P("graph", "feat"),
        P("feat", None),
        P(),
        P(),
        P(),
        P(("graph", "feat"), None, None, None),
        P(("graph", "feat"), None),
        P(("graph", "feat"), None, None),
        P(("graph", "feat"), None),
    )
    return jax.shard_map(
        shards, mesh=mesh, in_specs=placed, out_specs=P(("graph", "feat"), None), check_vma=False
    )
```

```python
import jax
import jax.numpy as jnp
from jax import lax
from jax.experimental import pallas as pl
from jax.experimental.pallas import tpu as pltpu
from jax.sharding import PartitionSpec as P

HEADS = 4
NT = (((1,), (1,)), ((), ()))


def split_bf16(x):
    hi = x.astype(jnp.bfloat16)
    lo = (x - hi.astype(jnp.float32)).astype(jnp.bfloat16)
    return hi, lo


def layer_kernel(
    send_ref,
    rels_ref,
    slots_ref,
    x_ref,
    w_ref,
    relw_ref,
    atts_ref,
    attt_ref,
    mask_ref,
    out_ref,
    tile,
    lists_got,
    lists_smem,
    spot,
    xin,
    xst,
    xg,
    wg,
    hid,
    stage,
    front,
    values,
    scores,
    satt,
    tatt,
    target,
    stack0,
    stack1,
    raws0,
    raws1,
    weights0,
    weights1,
    live,
    bias,
    local_sem,
    l_send,
    l_recv,
    w_send,
    w_recv,
    x_send,
    x_recv,
    z_send,
    z_recv,
):
    feats, blocks, rows, depth = x_ref.shape
    graphs, cap = send_ref.shape
    width = w_ref.shape[1]
    relations = relw_ref.shape[0]
    lists = mask_ref.shape[1]
    slots = graphs * cap
    hw = width // HEADS
    stack, raws, weights = (stack0, stack1), (raws0, raws1), (weights0, weights1)
    parts = ((0, cap), (cap, blocks - cap))
    g = lax.axis_index("graph")
    f = lax.axis_index("feat")
    mesh_id = pl.DeviceIdType.MESH
    parity = lax.rem(f, 2)

    def flip(index, bits, size):
        place, bit = 0, 1
        while bit < size:
            place = place + bit * ((index // bit + bits // bit) % 2)
            bit *= 2
        return place

    if feats == 8:
        even, odd = (2, 4, 6, 3, 5, 7, 1), (4, 2, 7, 5, 3, 6, 1)
    else:
        even = odd = tuple(range(1, feats))
    pairs = tuple(m for m in range(2, feats, 2))
    turns = tuple(pairs[1:2] + pairs[:1] + pairs[2:])

    def feat_at(n):
        return flip(f, even[n] + parity * (odd[n] - even[n]), feats)

    def same_core(n):
        return flip(f, pairs[n] + parity * (turns[n] - pairs[n]), feats)

    sib = f + 1 - 2 * parity
    others = range(feats - 1)
    chips = range(len(pairs))
    inner = jnp.logical_and(g > 0, g < graphs - 1)

    def graph_at(j):
        return flip(g, j, graphs)

    def order(n):
        return graphs - 1 - n + jnp.where(inner, 1 if n else 2 - graphs, 0)

    def w_rows(s):
        return wg.at[pl.ds(pl.multiple_of(s * depth, depth), depth)]

    def remote(src, dst, send_sem, recv_sem, where):
        return pltpu.make_async_remote_copy(
            src_ref=src,
            dst_ref=dst,
            send_sem=send_sem,
            recv_sem=recv_sem,
            device_id=where,
            device_id_type=mesh_id,
        )

    def w_direct(n):
        to = same_core(n) if n < len(pairs) else sib
        return remote(w_ref, w_rows(f), w_send.at[n], w_recv.at[f], {"feat": to})

    def w_relay(n):
        s = same_core(n)
        return remote(w_rows(s), w_rows(s), w_send.at[feats + n], w_recv.at[s], {"feat": sib})

    def piece(c):
        return pl.ds(*parts[c])

    def x_copy(n, c):
        to = feat_at(n)
        return remote(
            xst.at[to, piece(c)],
            xg.at[f, piece(c)],
            x_send.at[n, c],
            x_recv.at[f, c],
            {"feat": to},
        )

    def x_arrival(n, c):
        s = feat_at(n)
        return remote(
            xst.at[s, piece(c)],
            xg.at[s, piece(c)],
            x_send.at[n, c],
            x_recv.at[s, c],
            {"feat": s},
        )

    first = graph_at(order(0))

    def l_copy(n):
        to = feat_at(n)
        return remote(
            tile, lists_got.at[f], l_send.at[n], l_recv.at[f], {"feat": to}
        )

    def l_arrival(n):
        s = feat_at(n)
        return remote(
            tile, lists_got.at[s], l_send.at[n], l_recv.at[s], {"feat": s}
        )

    def z_first(c):
        j = order(0)
        return remote(
            hid.at[c], front.at[g, c], z_send.at[j, c], z_recv.at[g, c], {"graph": first}
        )

    def z_copy(j, c):
        to = graph_at(j)
        return remote(
            stage.at[j, c], front.at[g, c], z_send.at[j, c], z_recv.at[g, c], {"graph": to}
        )

    def z_arrival(j, c):
        q = graph_at(j)
        return remote(
            stage.at[j, c], front.at[q, c], z_send.at[j, c], z_recv.at[q, c], {"graph": q}
        )

    own = [
        pltpu.make_async_copy(w_ref, w_rows(f), local_sem.at[0]),
        pltpu.make_async_copy(x_ref, xin, local_sem.at[1]),
    ]
    lane = lax.broadcasted_iota(jnp.int32, tile.shape, 1)
    listed = jnp.zeros(tile.shape, jnp.int32)
    for c in range(cap):
        listed = jnp.where(lane == c, send_ref[first, c], listed)
    tile[...] = listed
    lists_got[f] = listed
    masks = pltpu.make_async_copy(mask_ref, live, local_sem.at[3])
    for copy in own:
        copy.start()
    barrier = pltpu.get_barrier_semaphore()
    for n in others:
        pl.semaphore_signal(barrier, inc=1, device_id={"feat": feat_at(n)}, device_id_type=mesh_id)
    for j in range(1, graphs):
        pl.semaphore_signal(barrier, inc=1, device_id={"graph": graph_at(j)}, device_id_type=mesh_id)
    pl.semaphore_wait(barrier, feats + graphs - 2)

    for n in others:
        l_copy(n).start()
    for n in range(len(pairs) + 1):
        w_direct(n).start()
    for copy in own:
        copy.wait()
    for n in others:
        l_arrival(n).wait_recv()
    to_smem = pltpu.make_async_copy(lists_got, lists_smem, local_sem.at[4])
    to_smem.start()
    to_smem.wait()

    def unlisted(s, block):
        used = 0
        for c in range(cap):
            used = used + jnp.where(lists_smem[s, 0, c] == block, 1, 0)
        return 1 - jnp.minimum(used, 1)

    def fill(s, c):
        if c == 0:
            for t in range(cap):
                xst[s, t] = xin[s, lists_smem[s, 0, t]]
        else:
            free = [unlisted(s, block) for block in range(blocks)]
            for t in range(blocks - cap):
                found, seen = 0, 0
                for block in range(blocks):
                    hit = jnp.where(seen == t, free[block], 0)
                    found = found + hit * block
                    seen = seen + free[block]
                xst[s, cap + t] = xin[s, jnp.minimum(found, blocks - 1)]

    for n in others:
        fill(feat_at(n), 0)
        x_copy(n, 0).start()
    for n in chips:
        w_relay(n).wait_recv()
        w_relay(n).start()
    for n in others:
        fill(feat_at(n), 1)
        x_copy(n, 1).start()
    for c in range(2):
        fill(f, c)
    seen = 0
    for block in range(blocks):
        place = 0
        for c in range(cap):
            place = place + jnp.where(lists_smem[f, 0, c] == block, c, 0)
        free = unlisted(f, block)
        spot[block] = jnp.minimum(place + free * (cap + seen), blocks - 1)
        seen = seen + free
    masks.start()

    head_of = lax.broadcasted_iota(jnp.int32, (8, width), 1) // hw
    row_of = lax.broadcasted_iota(jnp.int32, (8, width), 0)
    for r in range(relations):
        halves = [
            jnp.where(head_of == row_of, half_att.astype(jnp.float32), 0.0)
            for half_att in split_bf16(atts_ref[r : r + 1, :])
        ]
        satt[r] = jnp.concatenate(halves, axis=0).astype(jnp.bfloat16)
        for n, half_att in enumerate(split_bf16(attt_ref[r : r + 1, :])):
            tatt[n, r * rows : (r + 1) * rows, :] = jnp.broadcast_to(
                half_att.astype(jnp.float32), (rows, width)
            ).astype(jnp.bfloat16)

    masks.wait()

    def make_bias(b, carry):
        bias[b] = jnp.where(live[b] > 0, 0.0, -jnp.inf)
        return carry

    lax.fori_loop(0, blocks, make_bias, 0)
    for n in range(len(pairs) + 1):
        s = flip(sib, 2 * n, feats)
        remote(w_ref, w_rows(s), w_send.at[0], w_recv.at[s], {"feat": sib}).wait_recv()

    def project(c):
        size = parts[c][1]
        for n in others:
            x_arrival(n, c).wait_recv()
        xg[f, piece(c)] = xst[f, piece(c)]
        taken = jnp.concatenate(
            [xg[s, piece(c)].reshape(size * rows, depth) for s in range(feats)], axis=1
        )
        made = jnp.dot(taken, wg[...], preferred_element_type=jnp.float32)
        hid[piece(c)] = made.astype(hid.dtype).reshape(size, rows, width)

    for n in others:
        x_arrival(n, 0).wait_recv()
    xg[f, piece(0)] = xst[f, piece(0)]

    def project_one(c, carry):
        taken = jnp.concatenate([xg[s, c] for s in range(feats)], axis=1)
        made = jnp.dot(taken, wg[...], preferred_element_type=jnp.float32)
        hid[c] = made.astype(hid.dtype)
        z_first(c).start()
        return carry

    lax.fori_loop(0, cap, project_one, 0)
    project(1)
    for n in range(1, graphs - 1):
        j = order(n)
        to = graph_at(j)
        for c in range(cap):
            stage[j, c] = hid[spot[send_ref[to, c]]]
            z_copy(j, c).start()
    for c in range(cap):
        front[g, c] = hid[spot[send_ref[g, c]]]

    def score_targets(c):
        size = parts[c][1]
        mine = hid[piece(c)].reshape(size * rows, width)
        for h in range(HEADS):
            cols = slice(h * hw, (h + 1) * hw)
            both = lax.dot_general(
                mine[:, cols], tatt[0, :, cols], NT, preferred_element_type=jnp.float32
            ) + lax.dot_general(
                mine[:, cols], tatt[1, :, cols], NT, preferred_element_type=jnp.float32
            )
            for r in range(relations):
                target[h, r, piece(c)] = both[:, r * rows : (r + 1) * rows].reshape(
                    size, rows, rows
                )

    def transform(j):
        q = graph_at(j)
        taken = front[q].reshape(cap * rows, width)

        def relation(r, carry):
            v = jnp.dot(taken, relw_ref[r], preferred_element_type=jnp.float32)
            v = v.astype(jnp.bfloat16)
            both = lax.dot_general(satt[r], v, NT, preferred_element_type=jnp.float32)
            both = both[:8] + both[8:]
            for c in range(cap):
                values[r * slots + q * cap + c] = v[c * rows : (c + 1) * rows]
                scores[r * slots + q * cap + c] = both[:, c * rows : (c + 1) * rows]
            return carry

        lax.fori_loop(0, relations, relation, 0)

    transform(0)
    for c in range(2):
        score_targets(c)

    def receive(j, carry):
        for c in range(cap):
            z_arrival(j, c).wait_recv()
        transform(j)
        return carry

    lax.fori_loop(1, graphs, receive, 0)

    def attend(pair, carry):
        for u in range(2):
            attend_one(2 * pair + u, stack[u], raws[u], weights[u])
        return carry

    def attend_one(b, stacked, raw_buf, weight_buf):
        at = spot[b]
        index = []
        for k in range(lists):
            rel = rels_ref[b, k]
            index.append((rel, rel * slots + slots_ref[b, k]))
        for k in range(lists):
            stacked[k * rows : (k + 1) * rows, :] = values[index[k][1]]
        for m in range(HEADS // 2):
            totals = []
            pair = (2 * m, 2 * m + 1)
            tops = [None, None]
            for k in range(lists):
                rel, place = index[k]
                closed = bias[b, k]
                for n, h in enumerate(pair):
                    raw = (target[h, rel, at] + scores[place, h : h + 1, :]) + closed
                    raw_buf[h, k] = raw
                    tops[n] = raw if k == 0 else jnp.maximum(tops[n], raw)
            tops = [jnp.max(top, axis=1, keepdims=True) for top in tops]
            tops = [jnp.broadcast_to(jnp.maximum(top, 0.2 * top), (rows, rows)) for top in tops]
            for n, h in enumerate(pair):
                total = None
                for k in range(lists):
                    raw = raw_buf[h, k]
                    prob = jnp.exp(jnp.maximum(raw, 0.2 * raw) - tops[n])
                    total = prob if total is None else total + prob
                    weight_buf[h * rows : (h + 1) * rows, k * rows : (k + 1) * rows] = (
                        prob.astype(jnp.bfloat16)
                    )
                totals.append(jnp.sum(total, axis=1, keepdims=True))
            both = jnp.dot(
                weight_buf[2 * m * rows : (2 * m + 2) * rows, :],
                stacked[:, 2 * m * hw : (2 * m + 2) * hw],
                preferred_element_type=jnp.float32,
            )
            for n in range(2):
                cols = slice((2 * m + n) * hw, (2 * m + n + 1) * hw)
                summed = both[n * rows : (n + 1) * rows, n * hw : (n + 1) * hw]
                mixed = summed * (1.0 / totals[n]) + hid[at, :, cols].astype(jnp.float32)
                out_ref[b, :, cols] = jnp.where(
                    mixed > 0, mixed, jnp.exp(jnp.minimum(mixed, 0.0)) - 1.0
                ).astype(out_ref.dtype)

    lax.fori_loop(0, blocks // 2, attend, 0)

    for n in others:
        l_copy(n).wait_send()
        for c in range(2):
            x_copy(n, c).wait_send()
    for n in range(len(pairs) + 1):
        w_direct(n).wait_send()
    for n in chips:
        w_relay(n).wait_send()
    for j in range(1, graphs):
        for c in range(cap):
            z_copy(j, c).wait_send()


def layer(send, rels, slots, x, w, relw, atts, attt, mask):
    feats, blocks, rows, depth = x.shape
    width = w.shape[1]
    graphs, cap = send.shape
    lists = mask.shape[1]
    relations = relw.shape[0]
    count = relations * graphs * cap
    hw = width // HEADS
    dma = pltpu.SemaphoreType.DMA
    anywhere = pl.BlockSpec(memory_space=pl.ANY)
    whole = pl.BlockSpec(memory_space=pltpu.VMEM)
    smem = pl.BlockSpec(memory_space=pltpu.SMEM)
    bf16, f32 = jnp.bfloat16, jnp.float32
    return pl.pallas_call(
        layer_kernel,
        in_specs=[smem, smem, smem, anywhere, anywhere, whole, whole, whole, anywhere],
        out_specs=whole,
        out_shape=jax.ShapeDtypeStruct((blocks, rows, width), bf16),
        scratch_shapes=[
            pltpu.VMEM((8, 128), jnp.int32),
            pltpu.VMEM((feats, 8, 128), jnp.int32),
            pltpu.SMEM((feats, 8, 128), jnp.int32),
            pltpu.SMEM((blocks,), jnp.int32),
            pltpu.VMEM((feats, blocks, rows, depth), bf16),
            pltpu.VMEM((feats, blocks, rows, depth), bf16),
            pltpu.VMEM((feats, blocks, rows, depth), bf16),
            pltpu.VMEM((feats * depth, width), bf16),
            pltpu.VMEM((blocks, rows, width), bf16),
            pltpu.VMEM((graphs, cap, rows, width), bf16),
            pltpu.VMEM((graphs, cap, rows, width), bf16),
            pltpu.VMEM((count, rows, width), bf16),
            pltpu.VMEM((count, 8, rows), f32),
            pltpu.VMEM((relations, 16, width), bf16),
            pltpu.VMEM((2, relations * rows, width), bf16),
            pltpu.VMEM((HEADS, relations, blocks, rows, rows), f32),
            pltpu.VMEM((lists * rows, width), bf16),
            pltpu.VMEM((lists * rows, width), bf16),
            pltpu.VMEM((HEADS, lists, rows, rows), f32),
            pltpu.VMEM((HEADS, lists, rows, rows), f32),
            pltpu.VMEM((HEADS * rows, lists * rows), bf16),
            pltpu.VMEM((HEADS * rows, lists * rows), bf16),
            pltpu.VMEM(mask.shape, jnp.int32),
            pltpu.VMEM(mask.shape, f32),
            dma((5,)),
            dma((feats,)),
            dma((feats,)),
            dma((2 * feats,)),
            dma((feats,)),
            dma((feats, 2)),
            dma((feats, 2)),
            dma((graphs, cap)),
            dma((graphs, cap)),
        ],
        compiler_params=pltpu.CompilerParams(
            collective_id=0, has_side_effects=True, vmem_limit_bytes=58 << 20
        ),
        name="layer",
    )(send, rels, slots, x, w, relw, atts, attt, mask)


def shards(x, w, relw, atts, attt, mask, rels, send, slots):
    rows = mask.shape[-1]
    blocks = mask.shape[0]
    x = x.reshape(-1, blocks, rows, x.shape[1])
    out = layer(send[0], rels, slots, x, w, relw, atts, attt, mask)
    return out.reshape(blocks * rows, -1)


def solution(mesh):
    placed = (
        P("graph", "feat"),
        P("feat", None),
        P(),
        P(),
        P(),
        P(("graph", "feat"), None, None, None),
        P(("graph", "feat"), None),
        P(("graph", "feat"), None, None),
        P(("graph", "feat"), None),
    )
    return jax.shard_map(
        shards, mesh=mesh, in_specs=placed, out_specs=P(("graph", "feat"), None), check_vma=False
    )
```

```python
import jax
import jax.numpy as jnp
from jax import lax
from jax.experimental import pallas as pl
from jax.experimental.pallas import tpu as pltpu
from jax.sharding import PartitionSpec as P

HEADS = 4
NT = (((1,), (1,)), ((), ()))


def split_bf16(x):
    hi = x.astype(jnp.bfloat16)
    lo = (x - hi.astype(jnp.float32)).astype(jnp.bfloat16)
    return hi, lo


def layer_kernel(
    send_ref,
    rels_ref,
    slots_ref,
    x_ref,
    w_ref,
    relw_ref,
    atts_ref,
    attt_ref,
    mask_ref,
    out_ref,
    tile,
    lists_got,
    lists_smem,
    spot,
    xin,
    xst,
    xg,
    wg,
    hid,
    stage,
    front,
    values,
    scores,
    satt,
    tatt,
    target,
    stack0,
    stack1,
    raws0,
    raws1,
    weights0,
    weights1,
    live,
    bias,
    local_sem,
    l_send,
    l_recv,
    w_send,
    w_recv,
    x_send,
    x_recv,
    z_send,
    z_recv,
):
    feats, blocks, rows, depth = x_ref.shape
    graphs, cap = send_ref.shape
    width = w_ref.shape[1]
    relations = relw_ref.shape[0]
    lists = mask_ref.shape[1]
    slots = graphs * cap
    hw = width // HEADS
    stack, raws, weights = (stack0, stack1), (raws0, raws1), (weights0, weights1)
    parts = ((0, cap), (cap, blocks - cap))
    g = lax.axis_index("graph")
    f = lax.axis_index("feat")
    mesh_id = pl.DeviceIdType.MESH
    parity = lax.rem(f, 2)

    def flip(index, bits, size):
        place, bit = 0, 1
        while bit < size:
            place = place + bit * ((index // bit + bits // bit) % 2)
            bit *= 2
        return place

    if feats == 8:
        even, odd = (2, 4, 6, 3, 5, 7, 1), (4, 2, 7, 5, 3, 6, 1)
    else:
        even = odd = tuple(range(1, feats))
    pairs = tuple(m for m in range(2, feats, 2))
    turns = tuple(pairs[1:2] + pairs[:1] + pairs[2:])

    def feat_at(n):
        return flip(f, even[n] + parity * (odd[n] - even[n]), feats)

    def same_core(n):
        return flip(f, pairs[n] + parity * (turns[n] - pairs[n]), feats)

    sib = f + 1 - 2 * parity
    others = range(feats - 1)
    chips = range(len(pairs))
    inner = jnp.logical_and(g > 0, g < graphs - 1)

    def graph_at(j):
        return flip(g, j, graphs)

    def order(n):
        return jnp.where(inner, n + 1, graphs - 1 - n)

    def w_rows(s):
        return wg.at[pl.ds(pl.multiple_of(s * depth, depth), depth)]

    def remote(src, dst, send_sem, recv_sem, where):
        return pltpu.make_async_remote_copy(
            src_ref=src,
            dst_ref=dst,
            send_sem=send_sem,
            recv_sem=recv_sem,
            device_id=where,
            device_id_type=mesh_id,
        )

    def w_direct(n):
        to = same_core(n) if n < len(pairs) else sib
        return remote(w_ref, w_rows(f), w_send.at[n], w_recv.at[f], {"feat": to})

    def w_relay(n):
        s = same_core(n)
        return remote(w_rows(s), w_rows(s), w_send.at[feats + n], w_recv.at[s], {"feat": sib})

    def piece(c):
        return pl.ds(*parts[c])

    def x_copy(n, c):
        to = feat_at(n)
        return remote(
            xst.at[to, piece(c)],
            xg.at[f, piece(c)],
            x_send.at[n, c],
            x_recv.at[f, c],
            {"feat": to},
        )

    def x_arrival(n, c):
        s = feat_at(n)
        return remote(
            xst.at[s, piece(c)],
            xg.at[s, piece(c)],
            x_send.at[n, c],
            x_recv.at[s, c],
            {"feat": s},
        )

    first = graph_at(order(0))

    def l_copy(n):
        to = feat_at(n)
        return remote(
            tile, lists_got.at[f], l_send.at[n], l_recv.at[f], {"feat": to}
        )

    def l_arrival(n):
        s = feat_at(n)
        return remote(
            tile, lists_got.at[s], l_send.at[n], l_recv.at[s], {"feat": s}
        )

    def z_first(c):
        j = order(0)
        return remote(
            hid.at[c], front.at[g, c], z_send.at[j, c], z_recv.at[g, c], {"graph": first}
        )

    def z_copy(j, c):
        to = graph_at(j)
        return remote(
            stage.at[j, c], front.at[g, c], z_send.at[j, c], z_recv.at[g, c], {"graph": to}
        )

    def z_arrival(j, c):
        q = graph_at(j)
        return remote(
            stage.at[j, c], front.at[q, c], z_send.at[j, c], z_recv.at[q, c], {"graph": q}
        )

    own = [
        pltpu.make_async_copy(w_ref, w_rows(f), local_sem.at[0]),
        pltpu.make_async_copy(x_ref, xin, local_sem.at[1]),
    ]
    lane = lax.broadcasted_iota(jnp.int32, tile.shape, 1)
    listed = jnp.zeros(tile.shape, jnp.int32)
    for c in range(cap):
        listed = jnp.where(lane == c, send_ref[first, c], listed)
    tile[...] = listed
    lists_got[f] = listed
    masks = pltpu.make_async_copy(mask_ref, live, local_sem.at[3])
    for copy in own:
        copy.start()
    barrier = pltpu.get_barrier_semaphore()
    for n in others:
        pl.semaphore_signal(barrier, inc=1, device_id={"feat": feat_at(n)}, device_id_type=mesh_id)
    for j in range(1, graphs):
        pl.semaphore_signal(barrier, inc=1, device_id={"graph": graph_at(j)}, device_id_type=mesh_id)
    pl.semaphore_wait(barrier, feats + graphs - 2)

    for n in others:
        l_copy(n).start()
    for n in range(len(pairs) + 1):
        w_direct(n).start()
    for copy in own:
        copy.wait()
    for n in others:
        l_arrival(n).wait_recv()
    to_smem = pltpu.make_async_copy(lists_got, lists_smem, local_sem.at[4])
    to_smem.start()
    to_smem.wait()

    def unlisted(s, block):
        used = 0
        for c in range(cap):
            used = used + jnp.where(lists_smem[s, 0, c] == block, 1, 0)
        return 1 - jnp.minimum(used, 1)

    def fill(s, c):
        if c == 0:
            for t in range(cap):
                xst[s, t] = xin[s, lists_smem[s, 0, t]]
        else:
            free = [unlisted(s, block) for block in range(blocks)]
            for t in range(blocks - cap):
                found, seen = 0, 0
                for block in range(blocks):
                    hit = jnp.where(seen == t, free[block], 0)
                    found = found + hit * block
                    seen = seen + free[block]
                xst[s, cap + t] = xin[s, jnp.minimum(found, blocks - 1)]

    for n in others:
        fill(feat_at(n), 0)
        x_copy(n, 0).start()
    for n in chips:
        w_relay(n).wait_recv()
        w_relay(n).start()
    for n in others:
        fill(feat_at(n), 1)
        x_copy(n, 1).start()
    for c in range(2):
        fill(f, c)
    seen = 0
    for block in range(blocks):
        place = 0
        for c in range(cap):
            place = place + jnp.where(lists_smem[f, 0, c] == block, c, 0)
        free = unlisted(f, block)
        spot[block] = jnp.minimum(place + free * (cap + seen), blocks - 1)
        seen = seen + free
    masks.start()

    head_of = lax.broadcasted_iota(jnp.int32, (8, width), 1) // hw
    row_of = lax.broadcasted_iota(jnp.int32, (8, width), 0)
    for r in range(relations):
        halves = [
            jnp.where(head_of == row_of, half_att.astype(jnp.float32), 0.0)
            for half_att in split_bf16(atts_ref[r : r + 1, :])
        ]
        satt[r] = jnp.concatenate(halves, axis=0).astype(jnp.bfloat16)
        for n, half_att in enumerate(split_bf16(attt_ref[r : r + 1, :])):
            tatt[n, r * rows : (r + 1) * rows, :] = jnp.broadcast_to(
                half_att.astype(jnp.float32), (rows, width)
            ).astype(jnp.bfloat16)

    masks.wait()

    def make_bias(b, carry):
        bias[b] = jnp.where(live[b] > 0, 0.0, -jnp.inf)
        return carry

    lax.fori_loop(0, blocks, make_bias, 0)
    for n in range(len(pairs) + 1):
        s = flip(sib, 2 * n, feats)
        remote(w_ref, w_rows(s), w_send.at[0], w_recv.at[s], {"feat": sib}).wait_recv()

    def project(c):
        size = parts[c][1]
        for n in others:
            x_arrival(n, c).wait_recv()
        xg[f, piece(c)] = xst[f, piece(c)]
        taken = jnp.concatenate(
            [xg[s, piece(c)].reshape(size * rows, depth) for s in range(feats)], axis=1
        )
        made = jnp.dot(taken, wg[...], preferred_element_type=jnp.float32)
        hid[piece(c)] = made.astype(hid.dtype).reshape(size, rows, width)

    for n in others:
        x_arrival(n, 0).wait_recv()
    xg[f, piece(0)] = xst[f, piece(0)]

    def project_one(c, carry):
        taken = jnp.concatenate([xg[s, c] for s in range(feats)], axis=1)
        made = jnp.dot(taken, wg[...], preferred_element_type=jnp.float32)
        hid[c] = made.astype(hid.dtype)
        z_first(c).start()
        return carry

    lax.fori_loop(0, cap, project_one, 0)
    project(1)
    for n in range(1, graphs - 1):
        j = order(n)
        to = graph_at(j)
        for c in range(cap):
            stage[j, c] = hid[spot[send_ref[to, c]]]
            z_copy(j, c).start()
    for c in range(cap):
        front[g, c] = hid[spot[send_ref[g, c]]]

    def score_targets(c):
        size = parts[c][1]
        mine = hid[piece(c)].reshape(size * rows, width)
        for h in range(HEADS):
            cols = slice(h * hw, (h + 1) * hw)
            both = lax.dot_general(
                mine[:, cols], tatt[0, :, cols], NT, preferred_element_type=jnp.float32
            ) + lax.dot_general(
                mine[:, cols], tatt[1, :, cols], NT, preferred_element_type=jnp.float32
            )
            for r in range(relations):
                target[h, r, piece(c)] = both[:, r * rows : (r + 1) * rows].reshape(
                    size, rows, rows
                )

    def transform(j):
        q = graph_at(j)
        taken = front[q].reshape(cap * rows, width)

        def relation(r, carry):
            v = jnp.dot(taken, relw_ref[r], preferred_element_type=jnp.float32)
            v = v.astype(jnp.bfloat16)
            both = lax.dot_general(satt[r], v, NT, preferred_element_type=jnp.float32)
            both = both[:8] + both[8:]
            for c in range(cap):
                values[r * slots + q * cap + c] = v[c * rows : (c + 1) * rows]
                scores[r * slots + q * cap + c] = both[:, c * rows : (c + 1) * rows]
            return carry

        lax.fori_loop(0, relations, relation, 0)

    transform(0)
    for c in range(2):
        score_targets(c)

    def receive(j, carry):
        for c in range(cap):
            z_arrival(j, c).wait_recv()
        transform(j)
        return carry

    lax.fori_loop(1, graphs, receive, 0)

    def attend(pair, carry):
        for u in range(2):
            attend_one(2 * pair + u, stack[u], raws[u], weights[u])
        return carry

    def attend_one(b, stacked, raw_buf, weight_buf):
        at = spot[b]
        index = []
        for k in range(lists):
            rel = rels_ref[b, k]
            index.append((rel, rel * slots + slots_ref[b, k]))
        for k in range(lists):
            stacked[k * rows : (k + 1) * rows, :] = values[index[k][1]]
        for m in range(HEADS // 2):
            totals = []
            pair = (2 * m, 2 * m + 1)
            tops = [None, None]
            for k in range(lists):
                rel, place = index[k]
                closed = bias[b, k]
                for n, h in enumerate(pair):
                    raw = (target[h, rel, at] + scores[place, h : h + 1, :]) + closed
                    raw_buf[h, k] = raw
                    tops[n] = raw if k == 0 else jnp.maximum(tops[n], raw)
            tops = [jnp.max(top, axis=1, keepdims=True) for top in tops]
            tops = [jnp.broadcast_to(jnp.maximum(top, 0.2 * top), (rows, rows)) for top in tops]
            for n, h in enumerate(pair):
                total = None
                for k in range(lists):
                    raw = raw_buf[h, k]
                    prob = jnp.exp(jnp.maximum(raw, 0.2 * raw) - tops[n])
                    total = prob if total is None else total + prob
                    weight_buf[h * rows : (h + 1) * rows, k * rows : (k + 1) * rows] = (
                        prob.astype(jnp.bfloat16)
                    )
                totals.append(jnp.sum(total, axis=1, keepdims=True))
            both = jnp.dot(
                weight_buf[2 * m * rows : (2 * m + 2) * rows, :],
                stacked[:, 2 * m * hw : (2 * m + 2) * hw],
                preferred_element_type=jnp.float32,
            )
            for n in range(2):
                cols = slice((2 * m + n) * hw, (2 * m + n + 1) * hw)
                summed = both[n * rows : (n + 1) * rows, n * hw : (n + 1) * hw]
                mixed = summed * (1.0 / totals[n]) + hid[at, :, cols].astype(jnp.float32)
                out_ref[b, :, cols] = jnp.where(
                    mixed > 0, mixed, jnp.exp(jnp.minimum(mixed, 0.0)) - 1.0
                ).astype(out_ref.dtype)

    lax.fori_loop(0, blocks // 2, attend, 0)

    for n in others:
        l_copy(n).wait_send()
        for c in range(2):
            x_copy(n, c).wait_send()
    for n in range(len(pairs) + 1):
        w_direct(n).wait_send()
    for n in chips:
        w_relay(n).wait_send()
    for j in range(1, graphs):
        for c in range(cap):
            z_copy(j, c).wait_send()


def layer(send, rels, slots, x, w, relw, atts, attt, mask):
    feats, blocks, rows, depth = x.shape
    width = w.shape[1]
    graphs, cap = send.shape
    lists = mask.shape[1]
    relations = relw.shape[0]
    count = relations * graphs * cap
    hw = width // HEADS
    dma = pltpu.SemaphoreType.DMA
    anywhere = pl.BlockSpec(memory_space=pl.ANY)
    whole = pl.BlockSpec(memory_space=pltpu.VMEM)
    smem = pl.BlockSpec(memory_space=pltpu.SMEM)
    bf16, f32 = jnp.bfloat16, jnp.float32
    return pl.pallas_call(
        layer_kernel,
        in_specs=[smem, smem, smem, anywhere, anywhere, whole, whole, whole, anywhere],
        out_specs=whole,
        out_shape=jax.ShapeDtypeStruct((blocks, rows, width), bf16),
        scratch_shapes=[
            pltpu.VMEM((8, 128), jnp.int32),
            pltpu.VMEM((feats, 8, 128), jnp.int32),
            pltpu.SMEM((feats, 8, 128), jnp.int32),
            pltpu.SMEM((blocks,), jnp.int32),
            pltpu.VMEM((feats, blocks, rows, depth), bf16),
            pltpu.VMEM((feats, blocks, rows, depth), bf16),
            pltpu.VMEM((feats, blocks, rows, depth), bf16),
            pltpu.VMEM((feats * depth, width), bf16),
            pltpu.VMEM((blocks, rows, width), bf16),
            pltpu.VMEM((graphs, cap, rows, width), bf16),
            pltpu.VMEM((graphs, cap, rows, width), bf16),
            pltpu.VMEM((count, rows, width), bf16),
            pltpu.VMEM((count, 8, rows), f32),
            pltpu.VMEM((relations, 16, width), bf16),
            pltpu.VMEM((2, relations * rows, width), bf16),
            pltpu.VMEM((HEADS, relations, blocks, rows, rows), f32),
            pltpu.VMEM((lists * rows, width), bf16),
            pltpu.VMEM((lists * rows, width), bf16),
            pltpu.VMEM((HEADS, lists, rows, rows), f32),
            pltpu.VMEM((HEADS, lists, rows, rows), f32),
            pltpu.VMEM((HEADS * rows, lists * rows), bf16),
            pltpu.VMEM((HEADS * rows, lists * rows), bf16),
            pltpu.VMEM(mask.shape, jnp.int32),
            pltpu.VMEM(mask.shape, f32),
            dma((5,)),
            dma((feats,)),
            dma((feats,)),
            dma((2 * feats,)),
            dma((feats,)),
            dma((feats, 2)),
            dma((feats, 2)),
            dma((graphs, cap)),
            dma((graphs, cap)),
        ],
        compiler_params=pltpu.CompilerParams(
            collective_id=0, has_side_effects=True, vmem_limit_bytes=58 << 20
        ),
        name="layer",
    )(send, rels, slots, x, w, relw, atts, attt, mask)


def shards(x, w, relw, atts, attt, mask, rels, send, slots):
    rows = mask.shape[-1]
    blocks = mask.shape[0]
    x = x.reshape(-1, blocks, rows, x.shape[1])
    out = layer(send[0], rels, slots, x, w, relw, atts, attt, mask)
    return out.reshape(blocks * rows, -1)


def solution(mesh):
    placed = (
        P("graph", "feat"),
        P("feat", None),
        P(),
        P(),
        P(),
        P(("graph", "feat"), None, None, None),
        P(("graph", "feat"), None),
        P(("graph", "feat"), None, None),
        P(("graph", "feat"), None),
    )
    return jax.shard_map(
        shards, mesh=mesh, in_specs=placed, out_specs=P(("graph", "feat"), None), check_vma=False
    )
```
